32 devices in a mesh: wide: 8 (over y, x, core), narrow: 4 (over z).
Axes of the slice: x: 2, y: 2, z: 4, core: 2. Of those that a mesh axis runs over, the one named last changes fastest.
Arguments:
- tokens: bfloat16 [2048, 2048], P('wide', 'narrow'), may hold values from -6 to 6
- norm_gain: bfloat16 [2048], replicated, may hold values from 0.25 to 1.75
- router: bfloat16 [2048, 8], replicated, may hold values from -0.125 to 0.125
- routes: int32 [2048, 2], P('wide'), may hold values from 0 to 7, all different within a row
- kv_weight: bfloat16 [4096, 2048], P('narrow', 'wide'), may hold values from -0.125 to 0.125
- query_weight: bfloat16 [16384, 2048], P('narrow', 'wide'), may hold values from -0.125 to 0.125
- out_weight: bfloat16 [16384, 2048], P('narrow', 'wide'), may hold values from -0.09375 to 0.09375
- prefix_cache: bfloat16 [6144, 4096], P('wide', 'narrow'), may hold values from -225 to 225
- suffix_lengths: int32 [4], replicated, may hold values from 1 to 1280, 2048 in all
- prefix_lengths: int32 [4], replicated, may hold values from 1 to 3072, 6144 in all
Outputs:
- mixed: bfloat16 [2048, 2048], P('wide', 'narrow')
The draws below stay inside these ranges and needn't reach their ends.
Inputs may be any that keep to these rules, and one draw needn't show every extreme that they name: `routes`: each token names 2 different experts. `suffix_lengths`: they sum to 2048. `prefix_lengths`: they sum to 6144.
All inputs are finite; a program needn't handle non-finite values.
Results may differ from the reference program's by a relative error of at most 0.012.
The reference program's roundings to bfloat16 on the way (of `normed`, `kv_rows`, `query_all`, `selected` and `attended`) count: a program that leaves them out, or rounds other values in their place, can miss the bound.
Values may be sent and summed in bfloat16 or wider, within the bound.
A program may use at most 320 MiB of HBM per device.

```python
import math
import jax
import jax.numpy as jnp
import numpy as np
from jax import lax

D = 2048
KVH = 16
H = 128
E = 8
TOPK = 2
TENANTS = 4
TOK_DEV = 256
TOKENS = 2048
PREFIX = 6144


def draw_prefix_cache(key, part):
    values = jnp.clip(jax.random.normal(key, (PREFIX, KVH * 2 * H), jnp.float32), -4.5, 4.5)
    return values.astype(jnp.bfloat16)


def block_levels(key, dims, shards, low, largest):
    level, own = 1.0, jax.random.fold_in(key, 6)
    for axis_at, blocks in shards:
        heights = jnp.exp(jax.random.uniform(jax.random.fold_in(own, axis_at), (blocks,), jnp.float32, low / len(shards), largest / len(shards)))
        level = level * jnp.repeat(heights, dims[axis_at] // blocks).reshape([-1 if axis == axis_at else 1 for axis in range(len(dims))])
    return level


def distinct(rng, rows, number_of, top, lift):
    order = jax.random.permutation(jax.random.fold_in(rng, 1), number_of)
    favour = order
    for power in range(3):
        favour = favour * favour // number_of
    favour = favour * lift // number_of
    chance = jax.random.randint(jax.random.fold_in(rng, 2), (rows, number_of), 0, 4096) + favour
    holders = jax.random.permutation(jax.random.fold_in(rng, 3), rows)[jnp.arange(number_of) % rows]
    chance = jnp.where(jnp.arange(rows)[:, None] == holders[None, :], 1 << 14, chance)
    score = chance * number_of + jnp.arange(number_of)
    return lax.top_k(score.astype(jnp.int32), top)[1].astype(jnp.int32)


def length_profile(amount, total, bound, slope):
    portions = [(1 << 20) // math.isqrt(grade ** slope) + 1 for grade in range(2, amount + 1)]
    rest, holding = total - bound - (amount - 1), [1] * (amount - 1)
    while rest > 0:
        free = [i for i in range(amount - 1) if holding[i] < bound]
        whole, left = sum([portions[i] for i in free]), rest
        for i in free:
            more = min(bound - holding[i], max(1, left * portions[i] // whole), rest)
            holding[i] = holding[i] + more
            rest = rest - more
    return np.array([bound] + holding)


def ragged(stream_key, count, total, most, skew):
    if count == 2:
        one = jax.random.randint(stream_key, (), max(1, total - most), min(most, total - 1) + 1)
        return jnp.stack([one, total - one])
    tallies = jnp.asarray(length_profile(count, total, most, skew), jnp.int32)
    twos = (count - 1) // 2
    source_of, taker = tallies[1:1 + 2 * twos:2], tallies[2:2 + 2 * twos:2]
    room = jnp.minimum(source_of - 1, most - taker)
    moved = jax.random.randint(jax.random.fold_in(stream_key, 1), (twos,), 0, 1 << 20) % (room + 1)
    tallies = tallies.at[1:1 + 2 * twos:2].set(source_of - moved).at[2:2 + 2 * twos:2].set(taker + moved)
    return tallies[jax.random.permutation(jax.random.fold_in(stream_key, 2), count)]


def bell_draw(own_key, extent, scale, reach, pieces=(), kind=jnp.bfloat16):
    drawn = scale * jax.random.normal(own_key, extent, jnp.float32)
    if pieces:
        drawn = drawn * block_levels(own_key, extent, pieces, -0.22, 0.18)
    return jnp.clip(drawn, -reach, reach).astype(kind)


def setup_inputs(seed: int = 0) -> dict:
    key_of = jax.random.split(jax.random.key(seed), 11)
    return {
        "tokens": bell_draw(key_of[0], (TOKENS, D), 1.0, 6.0, ((0, 8), (1, 4))),
        "norm_gain": jnp.clip(1.0 + 0.15 * jax.random.normal(key_of[1], (D,), jnp.float32), 0.25, 1.75).astype(jnp.bfloat16),
        "router": bell_draw(key_of[2], (D, E), D ** -0.5, 0.125),
        "routes": distinct(key_of[3], TOKENS, E, TOPK, 2048),
        "kv_weight": bell_draw(key_of[4], (KVH * 2 * H, D), D ** -0.5, 0.125, ((0, 4), (1, 8))),
        "query_weight": bell_draw(key_of[5], (KVH * E * H, D), D ** -0.5, 0.125, ((0, 4), (1, 8))),
        "out_weight": bell_draw(key_of[6], (KVH * E * H, D), (TOPK * KVH * H) ** -0.5, 0.09375, ((0, 4), (1, 8))),
        "prefix_cache": draw_prefix_cache(jax.random.fold_in(key_of[10], 71), 0),
        "suffix_lengths": ragged(key_of[8], TENANTS, TOKENS, TOKENS - 3 * TOK_DEV, 2).astype(jnp.int32),
        "prefix_lengths": ragged(key_of[9], TENANTS, PREFIX, PREFIX // 2, 2).astype(jnp.int32),
    }


eps = 1e-06

def tenant_of(positions, lengths):
    bounds = jnp.cumsum(lengths).astype(jnp.int32)
    return lax.optimization_barrier(jnp.sum((positions[:, None] >= bounds[None, :]).astype(jnp.int32), axis=1)).astype(jnp.int32)

def reference(tokens, norm_gain, router, routes, kv_weight, query_weight, out_weight, prefix_cache, suffix_lengths, prefix_lengths):
    floats = tokens.astype(jnp.float32)
    normed = (floats * lax.rsqrt(lax.optimization_barrier(jnp.mean(floats * floats, axis=1, keepdims=True)) + eps) * norm_gain.astype(jnp.float32)).astype(jnp.bfloat16)
    logits = jnp.dot(normed, router, preferred_element_type=jnp.float32)
    choose = (routes[:, :, None] == jnp.arange(E, dtype=jnp.int32)[None, None, :]).astype(jnp.float32)
    chosen = lax.optimization_barrier(jnp.sum(choose * logits[:, None, :], axis=2))
    gate_values = jax.nn.softmax(chosen, axis=1)
    kv_rows = jnp.dot(normed, kv_weight.T, preferred_element_type=jnp.float32).astype(jnp.bfloat16).reshape(TOKENS, KVH, 2, H)
    query_all = jnp.dot(normed, query_weight.T, preferred_element_type=jnp.float32).astype(jnp.bfloat16).reshape(TOKENS, KVH, E, H)
    selected = jnp.einsum('tje,thed->thjd', choose, query_all.astype(jnp.float32)).astype(jnp.bfloat16)
    cache_rows = prefix_cache.reshape(PREFIX, KVH, 2, H)
    key_rows = jnp.concatenate([cache_rows[:, :, 0, :], kv_rows[:, :, 0, :]], axis=0)
    value_rows = jnp.concatenate([cache_rows[:, :, 1, :], kv_rows[:, :, 1, :]], axis=0)
    token_index = jnp.arange(TOKENS, dtype=jnp.int32)
    slot_index = jnp.arange(PREFIX, dtype=jnp.int32)
    token_tenant = tenant_of(token_index, suffix_lengths)
    slot_tenant = tenant_of(slot_index, prefix_lengths)
    prefix_allowed = token_tenant[:, None] == slot_tenant[None, :]
    suffix_allowed = (token_tenant[:, None] == token_tenant[None, :]) & (token_index[None, :] <= token_index[:, None])
    allowed = jnp.concatenate([prefix_allowed, suffix_allowed], axis=1)
    scaling = H ** (-0.5)

    def one_head(inputs):
        queries, keys_here, values_here = inputs
        scores = jnp.einsum('tjd,kd->tjk', queries.astype(jnp.float32), keys_here.astype(jnp.float32), precision=lax.Precision.HIGHEST) * scaling
        scores = jnp.where(allowed[:, None, :], scores, -jnp.inf)
        highest = lax.optimization_barrier(jnp.max(scores, axis=2, keepdims=True))
        weights = jnp.exp(scores - highest)
        totals = lax.optimization_barrier(jnp.sum(weights, axis=2))
        summed = jnp.einsum('tjk,kd->tjd', weights, values_here.astype(jnp.float32), precision=lax.Precision.HIGHEST)
        return summed / totals[:, :, None]
    attended = lax.map(one_head, (jnp.transpose(selected, (1, 0, 2, 3)), jnp.transpose(key_rows, (1, 0, 2)), jnp.transpose(value_rows, (1, 0, 2))))
    weighted = (attended * gate_values[None, :, :, None]).astype(jnp.bfloat16)
    padded = jnp.einsum('tje,htjd->thed', choose, weighted.astype(jnp.float32)).astype(jnp.bfloat16).reshape(TOKENS, KVH * E * H)
    return jnp.dot(padded, out_weight, preferred_element_type=jnp.float32).astype(jnp.bfloat16)
```

```python
import functools
import math

import jax
import jax.numpy as jnp
from jax import lax
from jax.experimental import pallas as pl
from jax.experimental.pallas import tpu as pltpu
from jax.sharding import PartitionSpec as P

H = 128
E = 8
EPS = 1e-06
FLOOR = -1e30
F32 = jnp.float32
BF16 = jnp.bfloat16
NT = (((1,), (1,)), ((), ()))
TN = (((0,), (0,)), ((), ()))


def pick(routes_column, blocks):
    found = jnp.zeros_like(blocks[0])
    for expert, block in enumerate(blocks):
        found = jnp.where(routes_column == expert, block, found)
    return found


def attend_kernel(
    group, suffix_ref, prefix_ref, sub_ref, normed_ref, router_ref, query_ref, routes_ref,
    cache_ref, kv_ref, out_ref
):
    block = normed_ref.shape[0]
    tenants = suffix_ref.shape[0]
    cache_rows = cache_ref.shape[0]
    cache_block = math.gcd(cache_rows, 512)
    strands = kv_ref.shape[0] // (group * block)
    token_block = pl.program_id(0) * group + sub_ref[0]
    first = token_block * block
    last = first + block - 1

    normed = normed_ref[...]
    logits = jnp.dot(normed, router_ref[...], preferred_element_type=F32)
    expert_at = lax.broadcasted_iota(jnp.int32, logits.shape, 1)
    route_a, route_b = routes_ref[:, 0:1], routes_ref[:, 1:2]
    logit_a = jnp.sum(jnp.where(expert_at == route_a, logits, 0.0), axis=1, keepdims=True)
    logit_b = jnp.sum(jnp.where(expert_at == route_b, logits, 0.0), axis=1, keepdims=True)
    top = jnp.maximum(logit_a, logit_b)
    up_a, up_b = jnp.exp(logit_a - top), jnp.exp(logit_b - top)
    gate_a, gate_b = up_a / (up_a + up_b), up_b / (up_a + up_b)

    every = lax.dot_general(normed, query_ref[...], NT, preferred_element_type=F32)
    parts = [every[:, e * H:(e + 1) * H] for e in range(E)]
    queries = jnp.concatenate([pick(route_a, parts), pick(route_b, parts)], axis=0).astype(BF16)

    token = first + lax.broadcasted_iota(jnp.int32, (1, block), 1)
    low = jnp.zeros((1, block), jnp.int32)
    high = jnp.zeros((1, block), jnp.int32)
    start = jnp.zeros((1, block), jnp.int32)
    low_block = jnp.int32(0)
    high_block = jnp.int32(0)
    start_block = jnp.int32(0)
    suffix_at = jnp.int32(0)
    prefix_at = jnp.int32(0)
    for tenant in range(tenants):
        suffix_end = suffix_at + suffix_ref[tenant]
        prefix_end = prefix_at + prefix_ref[tenant]
        inside = (token >= suffix_at) & (token < suffix_end)
        low = jnp.where(inside, prefix_at, low)
        high = jnp.where(inside, prefix_end, high)
        start = jnp.where(inside, suffix_at, start)
        holds_first = (first >= suffix_at) & (first < suffix_end)
        holds_last = (last >= suffix_at) & (last < suffix_end)
        low_block = jnp.where(holds_first, prefix_at, low_block)
        start_block = jnp.where(holds_first, suffix_at, start_block)
        high_block = jnp.where(holds_last, prefix_end, high_block)
        suffix_at, prefix_at = suffix_end, prefix_end
    twice = lambda row: jnp.concatenate([row, row], axis=1)
    low, high, start, upto = twice(low), twice(high), twice(start), twice(token + 1)
    to_log2 = math.log2(math.e) * H ** (-0.5)
    rows = 2 * block

    def over(carried, keys, values, key_first, row_low, row_high):
        highest, totals, summed = carried
        scores = lax.dot_general(keys, queries, NT, preferred_element_type=F32)
        at = key_first + lax.broadcasted_iota(jnp.int32, scores.shape, 0)
        scores = jnp.where((at >= row_low) & (at < row_high), scores, -jnp.inf)
        new_highest = jnp.maximum(highest, jnp.max(scores, axis=0, keepdims=True))
        weights = jnp.exp2((scores - new_highest) * to_log2)
        factor = jnp.exp2((highest - new_highest) * to_log2)
        totals = totals * factor + jnp.sum(weights, axis=0, keepdims=True)
        summed = summed * factor + lax.dot_general(
            values, weights.astype(BF16), TN, preferred_element_type=F32
        )
        return new_highest, totals, summed

    def over_cache(step, carried):
        at = pl.multiple_of(step * cache_block, cache_block)
        here = cache_ref[pl.ds(at, cache_block), :]
        return over(carried, here[:, :H], here[:, H:], at, low, high)

    def over_suffix(step, carried):
        place = lax.rem(step, group) * strands + lax.div(step, group)
        here = kv_ref[pl.ds(pl.multiple_of(place * block, block), block), :]
        return over(carried, here[:, :H], here[:, H:], step * block, start, upto)

    carried = (
        jnp.full((1, rows), FLOOR, F32),
        jnp.zeros((1, rows), F32),
        jnp.zeros((H, rows), F32),
    )
    carried = lax.fori_loop(
        lax.div(low_block, cache_block),
        lax.div(high_block + cache_block - 1, cache_block),
        over_cache,
        carried,
    )
    carried = lax.fori_loop(lax.div(start_block, block), token_block + 1, over_suffix, carried)
    unused, totals, summed = carried
    attended = jnp.transpose(summed / totals)
    out_ref[0] = (attended[:block] * gate_a).astype(BF16)
    out_ref[1] = (attended[block:] * gate_b).astype(BF16)


def out_kernel(attended_ref, weight_ref, routes_ref, out_ref):
    heads = attended_ref.shape[0]
    route_a, route_b = routes_ref[:, 0:1], routes_ref[:, 1:2]
    total = jnp.zeros(out_ref.shape, F32)
    for head in range(heads):
        first, second = attended_ref[head, 0, 0], attended_ref[head, 0, 1]
        nothing = jnp.zeros_like(first)
        padded = jnp.concatenate(
            [
                jnp.where(route_a == e, first, jnp.where(route_b == e, second, nothing))
                for e in range(E)
            ],
            axis=1,
        )
        total = total + jnp.dot(
            padded, weight_ref[head * E * H:(head + 1) * E * H, :], preferred_element_type=F32
        )
    out_ref[...] = total


def on_device(
    wide,
    narrow,
    tokens,
    norm_gain,
    router,
    routes,
    kv_weight,
    query_weight,
    out_weight,
    prefix_cache,
    suffix_lengths,
    prefix_lengths,
):
    block = tokens.shape[0]
    width = router.shape[0]
    heads = kv_weight.shape[0] // (2 * H)
    group = wide // heads
    strands = wide // group
    columns = width // wide
    me = lax.axis_index("wide")
    sub = lax.rem(me, group)
    same_sub = [[s + group * a for a in range(strands)] for s in range(group)]
    same_head = [[a * group + s for s in range(group)] for a in range(strands)]

    whole = lax.all_gather(tokens, "narrow", axis=1, tiled=True)
    floats = whole.astype(F32)
    normed = (
        floats
        * lax.rsqrt(jnp.mean(floats * floats, axis=1, keepdims=True) + EPS)
        * norm_gain.astype(F32)
    ).astype(BF16)
    normed = lax.all_gather(normed, "wide", axis_index_groups=same_sub, axis=0, tiled=True)
    routes_all = lax.all_gather(routes, "wide", axis=0, tiled=True)
    routes_here = lax.dynamic_slice_in_dim(
        routes_all.reshape(strands, group, block, 2), sub, 1, axis=1
    ).reshape(strands * block, 2)

    def spread(weight):
        mine = lax.all_to_all(weight, "wide", split_axis=0, concat_axis=1, tiled=True)
        return lax.all_gather(mine, "wide", axis_index_groups=same_head, axis=0, tiled=True)

    kv_rows = spread(kv_weight)
    query_rows = spread(query_weight)
    cache = lax.all_to_all(prefix_cache, "wide", split_axis=1, concat_axis=0, tiled=True)
    cache = lax.all_gather(cache, "wide", axis_index_groups=same_head, axis=1, tiled=True)

    kv = lax.dot_general(normed, kv_rows, NT, preferred_element_type=F32).astype(BF16)
    kv = lax.all_gather(kv, "wide", axis_index_groups=same_head, axis=0, tiled=True)

    whole_block = lambda array: pl.BlockSpec(array.shape, lambda i: (0,) * array.ndim)
    smem = pl.BlockSpec(memory_space=pltpu.SMEM)
    attended = pl.pallas_call(
        functools.partial(attend_kernel, group),
        grid=(strands,),
        out_shape=jax.ShapeDtypeStruct((2, strands * block, H), BF16),
        in_specs=[
            smem,
            smem,
            smem,
            pl.BlockSpec((block, width), lambda i: (i, 0)),
            whole_block(router),
            whole_block(query_rows),
            pl.BlockSpec((block, 2), lambda i: (i, 0)),
            whole_block(cache),
            whole_block(kv),
        ],
        out_specs=pl.BlockSpec((2, block, H), lambda i: (0, i, 0)),
        compiler_params=pltpu.CompilerParams(vmem_limit_bytes=56 * 1024 * 1024),
        name="attend",
    )(
        suffix_lengths, prefix_lengths, sub[None], normed, router, query_rows, routes_here, cache, kv
    )
    attended = lax.all_gather(attended, "wide", axis=0).reshape(
        heads, group, 2, strands * block, H
    )
    partial_out = pl.pallas_call(
        out_kernel,
        grid=(wide,),
        out_shape=jax.ShapeDtypeStruct((wide * block, columns), F32),
        in_specs=[
            pl.BlockSpec(
                (heads, 1, 2, block, H), lambda i: (0, lax.rem(i, group), 0, lax.div(i, group), 0)
            ),
            whole_block(out_weight),
            pl.BlockSpec((block, 2), lambda i: (i, 0)),
        ],
        out_specs=pl.BlockSpec((block, columns), lambda i: (i, 0)),
        compiler_params=pltpu.CompilerParams(vmem_limit_bytes=56 * 1024 * 1024),
        name="project_out",
    )(attended, out_weight, routes_all)
    mine = lax.psum_scatter(partial_out, "narrow", scatter_dimension=0, tiled=True).astype(BF16)
    ratio = wide // narrow
    mine = mine.reshape(ratio, block, columns)
    which = lax.rem(me, ratio)
    pieces = []
    for turn in range(ratio):
        chosen = lax.dynamic_index_in_dim(mine, lax.rem(which + turn, ratio), 0, keepdims=False)
        pairs = []
        for w in range(wide):
            for n in range(narrow):
                to_wide = ratio * n + (w % ratio + turn) % ratio
                to_narrow = w // ratio
                pairs.append((w * narrow + n, to_wide * narrow + to_narrow))
        pieces.append(lax.ppermute(chosen, ("wide", "narrow"), pairs))
    stacked = jnp.stack(pieces)
    ordered = [
        lax.dynamic_index_in_dim(stacked, lax.rem(which - k + ratio, ratio), 0, keepdims=False)
        for k in range(ratio)
    ]
    return jnp.concatenate(ordered, axis=1)


def solution(mesh):
    placed = (
        P("wide", "narrow"),
        P(),
        P(),
        P("wide", None),
        P("narrow", "wide"),
        P("narrow", "wide"),
        P("narrow", "wide"),
        P("wide", "narrow"),
        P(),
        P(),
    )
    return jax.shard_map(
        functools.partial(on_device, mesh.shape["wide"], mesh.shape["narrow"]),
        mesh=mesh,
        in_specs=placed,
        out_specs=P("wide", "narrow"),
        check_vma=False,
    )
```

```python
import functools
import math

import jax
import jax.numpy as jnp
from jax import lax
from jax.experimental import pallas as pl
from jax.experimental.pallas import tpu as pltpu
from jax.sharding import PartitionSpec as P

H = 128
E = 8
EPS = 1e-06
FLOOR = -1e30
F32 = jnp.float32
BF16 = jnp.bfloat16
NT = (((1,), (1,)), ((), ()))
TN = (((0,), (0,)), ((), ()))


def pick(routes_column, blocks):
    found = jnp.zeros_like(blocks[0])
    for expert, block in enumerate(blocks):
        found = jnp.where(routes_column == expert, block, found)
    return found


def route_columns(routes_rows):
    turned = jnp.transpose(routes_rows)
    return turned[:, 0:1], turned[:, 1:2]


def attend_kernel(
    group, suffix_ref, prefix_ref, sub_ref, normed_ref, router_ref, query_ref, routes_ref,
    cache_ref, kv_ref, out_ref
):
    block = normed_ref.shape[0]
    tenants = suffix_ref.shape[0]
    cache_rows = cache_ref.shape[0]
    cache_block = math.gcd(cache_rows, 512)
    strands = kv_ref.shape[0] // (group * block)
    token_block = pl.program_id(0) * group + sub_ref[0]
    first = token_block * block
    last = first + block - 1

    normed = normed_ref[...]
    logits = jnp.dot(normed, router_ref[...], preferred_element_type=F32)
    expert_at = lax.broadcasted_iota(jnp.int32, logits.shape, 1)
    route_a, route_b = route_columns(routes_ref[token_block])
    logit_a = jnp.sum(jnp.where(expert_at == route_a, logits, 0.0), axis=1, keepdims=True)
    logit_b = jnp.sum(jnp.where(expert_at == route_b, logits, 0.0), axis=1, keepdims=True)
    top = jnp.maximum(logit_a, logit_b)
    up_a, up_b = jnp.exp(logit_a - top), jnp.exp(logit_b - top)
    gate_a, gate_b = up_a / (up_a + up_b), up_b / (up_a + up_b)

    every = lax.dot_general(normed, query_ref[...], NT, preferred_element_type=F32)
    parts = [every[:, e * H:(e + 1) * H] for e in range(E)]
    queries = jnp.concatenate([pick(route_a, parts), pick(route_b, parts)], axis=0).astype(BF16)

    token = first + lax.broadcasted_iota(jnp.int32, (1, block), 1)
    low = jnp.zeros((1, block), jnp.int32)
    high = jnp.zeros((1, block), jnp.int32)
    start = jnp.zeros((1, block), jnp.int32)
    low_block = jnp.int32(0)
    high_block = jnp.int32(0)
    start_block = jnp.int32(0)
    suffix_at = jnp.int32(0)
    prefix_at = jnp.int32(0)
    for tenant in range(tenants):
        suffix_end = suffix_at + suffix_ref[tenant]
        prefix_end = prefix_at + prefix_ref[tenant]
        inside = (token >= suffix_at) & (token < suffix_end)
        low = jnp.where(inside, prefix_at, low)
        high = jnp.where(inside, prefix_end, high)
        start = jnp.where(inside, suffix_at, start)
        holds_first = (first >= suffix_at) & (first < suffix_end)
        holds_last = (last >= suffix_at) & (last < suffix_end)
        low_block = jnp.where(holds_first, prefix_at, low_block)
        start_block = jnp.where(holds_first, suffix_at, start_block)
        high_block = jnp.where(holds_last, prefix_end, high_block)
        suffix_at, prefix_at = suffix_end, prefix_end
    twice = lambda row: jnp.concatenate([row, row], axis=1)
    low, high, start, upto = twice(low), twice(high), twice(start), twice(token + 1)
    to_log2 = math.log2(math.e) * H ** (-0.5)
    rows = 2 * block

    def over(carried, keys, values, key_first, row_low, row_high):
        highest, totals, summed = carried
        scores = lax.dot_general(keys, queries, NT, preferred_element_type=F32)
        at = key_first + lax.broadcasted_iota(jnp.int32, scores.shape, 0)
        scores = jnp.where((at >= row_low) & (at < row_high), scores, -jnp.inf)
        new_highest = jnp.maximum(highest, jnp.max(scores, axis=0, keepdims=True))
        weights = jnp.exp2((scores - new_highest) * to_log2)
        factor = jnp.exp2((highest - new_highest) * to_log2)
        totals = totals * factor + jnp.sum(weights, axis=0, keepdims=True)
        summed = summed * factor + lax.dot_general(
            values, weights.astype(BF16), TN, preferred_element_type=F32
        )
        return new_highest, totals, summed

    def over_cache(step, carried):
        at = pl.multiple_of(step * cache_block, cache_block)
        here = cache_ref[pl.ds(at, cache_block), :]
        return over(carried, here[:, :H], here[:, H:], at, low, high)

    def over_suffix(step, carried):
        place = lax.rem(step, group) * strands + lax.div(step, group)
        here = kv_ref[pl.ds(pl.multiple_of(place * block, block), block), :]
        return over(carried, here[:, :H], here[:, H:], step * block, start, upto)

    carried = (
        jnp.full((1, rows), FLOOR, F32),
        jnp.zeros((1, rows), F32),
        jnp.zeros((H, rows), F32),
    )
    carried = lax.fori_loop(
        lax.div(low_block, cache_block),
        lax.div(high_block + cache_block - 1, cache_block),
        over_cache,
        carried,
    )
    carried = lax.fori_loop(lax.div(start_block, block), token_block + 1, over_suffix, carried)
    unused, totals, summed = carried
    attended = jnp.transpose(summed / totals)
    out_ref[0, 0] = (attended[:block] * gate_a).astype(BF16)
    out_ref[0, 1] = (attended[block:] * gate_b).astype(BF16)


def remote(source, target, send_sem, recv_sem, place):
    return pltpu.make_async_remote_copy(
        src_ref=source,
        dst_ref=target,
        send_sem=send_sem,
        recv_sem=recv_sem,
        device_id=place,
        device_id_type=pl.DeviceIdType.MESH,
    )


def greet(place):
    pl.semaphore_signal(
        pltpu.get_barrier_semaphore(),
        inc=1,
        device_id=place,
        device_id_type=pl.DeviceIdType.MESH,
    )


def finish_kernel(
    wide, narrow, group, attended_ref, weight_ref, routes_ref, out_ref,
    gathered, parts, got, mine, final,
    ring_send, ring_recv, pair_send, pair_recv, pass_send, pass_recv,
    deep_send, deep_recv, turn_send, turn_recv
):
    heads = wide // group
    ratio = wide // narrow
    block = attended_ref.shape[2]
    columns = weight_ref.shape[1]
    me, depth = lax.axis_index("wide"), lax.axis_index("narrow")
    head, sub = lax.div(me, group), lax.rem(me, group)
    turned = lax.div(me, ratio)
    lane = lax.rem(me, ratio)

    for k in range(1, wide):
        greet((lax.rem(me + k, wide), depth))
    for k in range(1, narrow):
        greet((me, lax.rem(depth + k, narrow)))
    for u in range(ratio):
        @pl.when(jnp.logical_or(ratio * depth + u != me, turned != depth))
        def _():
            greet((ratio * depth + u, turned))
    own_turn = (turned == depth).astype(jnp.int32)
    pl.semaphore_wait(pltpu.get_barrier_semaphore(), wide - 1 + narrow - 1 + ratio - own_turn)

    strand_at = [lax.rem(depth + 1 + k, heads) for k in range(heads)]
    sibling = [head * group + lax.rem(sub + ks, group) for ks in range(group)]

    def ring(k, ka):
        i = strand_at[k]
        other = lax.rem(head + ka, heads) * group + sub
        return remote(
            attended_ref.at[i], gathered.at[head, sub, i],
            ring_send.at[k, ka], ring_recv.at[k, ka], (other, depth)
        )

    def ring_in(k, ka):
        i = strand_at[k]
        source = lax.rem(head + heads - ka, heads)
        return remote(
            attended_ref.at[i], gathered.at[source, sub, i],
            ring_send.at[k, ka], ring_recv.at[k, ka], (source * group + sub, depth)
        )

    def pair(k, ks):
        i = strand_at[k]
        return remote(
            attended_ref.at[i], gathered.at[head, sub, i],
            pair_send.at[k, ks], pair_recv.at[k, ks], (sibling[ks], depth)
        )

    def pair_in(k, ks):
        i = strand_at[k]
        return remote(
            attended_ref.at[i], gathered.at[head, lax.rem(sub + group - ks, group), i],
            pair_send.at[k, ks], pair_recv.at[k, ks], (sibling[ks], depth)
        )

    def hand(k, ka, ks):
        i = strand_at[k]
        held = gathered.at[lax.rem(head + heads - ka, heads), sub, i]
        return remote(held, held, pass_send.at[k, ka, ks], pass_recv.at[k, ka, ks], (sibling[ks], depth))

    def hand_in(k, ka, ks):
        i = strand_at[k]
        held = gathered.at[
            lax.rem(head + heads - ka, heads), lax.rem(sub + group - ks, group), i
        ]
        return remote(held, held, pass_send.at[k, ka, ks], pass_recv.at[k, ka, ks], (sibling[ks], depth))

    for k in range(heads):
        for ka in range(1, heads):
            ring(k, ka).start()
        for ks in range(1, group):
            pair(k, ks).start()
    for k in range(heads):
        gathered[head, sub, strand_at[k]] = attended_ref[strand_at[k]]

    def stage(k):
        for ka in range(1, heads):
            ring_in(k, ka).wait_recv()
            for ks in range(1, group):
                hand(k, ka, ks).start()

    def arrive(k):
        for ks in range(1, group):
            pair_in(k, ks).wait_recv()
            for ka in range(1, heads):
                hand_in(k, ka, ks).wait_recv()

    def project(which):
        route_a, route_b = route_columns(routes_ref[which])
        total = jnp.zeros((block, columns), F32)
        for h in range(heads):
            first = gathered[h, lax.rem(which, group), lax.div(which, group), 0]
            second = gathered[h, lax.rem(which, group), lax.div(which, group), 1]
            nothing = jnp.zeros_like(first)
            padded = jnp.concatenate(
                [
                    jnp.where(route_a == e, first, jnp.where(route_b == e, second, nothing))
                    for e in range(E)
                ],
                axis=1,
            )
            total = total + jnp.dot(
                padded, weight_ref[h * E * H:(h + 1) * E * H, :], preferred_element_type=F32
            )
        return total

    def deep(k):
        to = lax.rem(depth + 1 + k, narrow)
        return remote(parts.at[k], got.at[k], deep_send.at[k], deep_recv.at[k], (me, to))

    one_each = narrow == heads
    if one_each:
        stage(0)
    else:
        for k in range(heads):
            stage(k)
        for k in range(heads):
            arrive(k)
    owned = []
    for k in range(narrow):
        if one_each:
            if k + 1 < heads:
                stage(k + 1)
            arrive(k)
        quarter = lax.rem(depth + 1 + k, narrow)
        for u in range(ratio):
            total = project(quarter * ratio + u)
            if k < narrow - 1:
                parts[k, u] = total.astype(BF16)
            else:
                owned.append(total)
        if k < narrow - 1:
            deep(k).start()
    for k in range(narrow - 1):
        deep(k).wait_recv()
    for u in range(ratio):
        total = owned[u]
        for k in range(narrow - 1):
            total = total + got[k, u].astype(F32)
        mine[u] = total.astype(BF16)

    def turn(u):
        return remote(
            mine.at[u], final.at[lane], turn_send.at[u], turn_recv.at[lane],
            (ratio * depth + u, turned)
        )

    def turn_in(u):
        return remote(
            mine.at[u], final.at[u], turn_send.at[u], turn_recv.at[u],
            (ratio * depth + u, turned)
        )

    for u in range(ratio):
        apart = jnp.logical_or(ratio * depth + u != me, turned != depth)

        @pl.when(apart)
        def _():
            turn(u).start()

        @pl.when(jnp.logical_not(apart))
        def _():
            final[lane] = mine[u]

    for u in range(ratio):
        apart = jnp.logical_or(ratio * depth + u != me, turned != depth)

        @pl.when(apart)
        def _():
            turn_in(u).wait_recv()

        out_ref[:, u * columns:(u + 1) * columns] = final[u]

    for k in range(heads):
        for ka in range(1, heads):
            ring(k, ka).wait_send()
            for ks in range(1, group):
                hand(k, ka, ks).wait_send()
        for ks in range(1, group):
            pair(k, ks).wait_send()
    for k in range(narrow - 1):
        deep(k).wait_send()
    for u in range(ratio):
        @pl.when(jnp.logical_or(ratio * depth + u != me, turned != depth))
        def _():
            turn(u).wait_send()


def on_device(
    wide,
    narrow,
    tokens,
    norm_gain,
    router,
    routes,
    kv_weight,
    query_weight,
    out_weight,
    prefix_cache,
    suffix_lengths,
    prefix_lengths,
):
    block = tokens.shape[0]
    width = router.shape[0]
    heads = kv_weight.shape[0] // (2 * H)
    group = wide // heads
    strands = wide // group
    columns = width // wide
    me = lax.axis_index("wide")
    sub = lax.rem(me, group)
    same_sub = [[s + group * a for a in range(strands)] for s in range(group)]
    same_head = [[a * group + s for s in range(group)] for a in range(strands)]

    whole = lax.all_gather(tokens, "narrow", axis=1, tiled=True)
    floats = whole.astype(F32)
    normed = (
        floats
        * lax.rsqrt(jnp.mean(floats * floats, axis=1, keepdims=True) + EPS)
        * norm_gain.astype(F32)
    ).astype(BF16)
    normed = lax.all_gather(normed, "wide", axis_index_groups=same_sub, axis=0, tiled=True)
    routes_all = lax.all_gather(
        jnp.pad(jnp.transpose(routes), ((0, 6), (0, 0))), "wide", axis=0
    )

    def spread(weight):
        mine = lax.all_to_all(weight, "wide", split_axis=0, concat_axis=1, tiled=True)
        return lax.all_gather(mine, "wide", axis_index_groups=same_head, axis=0, tiled=True)

    kv_rows = spread(kv_weight)
    query_rows = spread(query_weight)
    cache = lax.all_to_all(prefix_cache, "wide", split_axis=1, concat_axis=0, tiled=True)
    cache = lax.all_gather(cache, "wide", axis_index_groups=same_head, axis=1, tiled=True)

    kv = lax.dot_general(normed, kv_rows, NT, preferred_element_type=F32).astype(BF16)
    kv = lax.all_gather(kv, "wide", axis_index_groups=same_head, axis=0, tiled=True)

    whole_block = lambda array: pl.BlockSpec(array.shape, lambda i: (0,) * array.ndim)
    smem = pl.BlockSpec(memory_space=pltpu.SMEM)
    attended = pl.pallas_call(
        functools.partial(attend_kernel, group),
        grid=(strands,),
        out_shape=jax.ShapeDtypeStruct((strands, 2, block, H), BF16),
        in_specs=[
            smem,
            smem,
            smem,
            pl.BlockSpec((block, width), lambda i: (i, 0)),
            whole_block(router),
            whole_block(query_rows),
            whole_block(routes_all),
            whole_block(cache),
            whole_block(kv),
        ],
        out_specs=pl.BlockSpec((1, 2, block, H), lambda i: (i, 0, 0, 0)),
        compiler_params=pltpu.CompilerParams(vmem_limit_bytes=56 * 1024 * 1024),
        name="attend",
    )(
        suffix_lengths, prefix_lengths, sub[None], normed, router, query_rows, routes_all, cache, kv
    )
    ratio = wide // narrow
    in_vmem = pl.BlockSpec(memory_space=pltpu.VMEM)
    dma = pltpu.SemaphoreType.DMA
    return pl.pallas_call(
        functools.partial(finish_kernel, wide, narrow, group),
        out_shape=jax.ShapeDtypeStruct((block, ratio * columns), BF16),
        in_specs=[in_vmem] * 3,
        out_specs=in_vmem,
        scratch_shapes=[
            pltpu.VMEM((heads, group, strands, 2, block, H), BF16),
            pltpu.VMEM((narrow - 1, ratio, block, columns), BF16),
            pltpu.VMEM((narrow - 1, ratio, block, columns), BF16),
            pltpu.VMEM((ratio, block, columns), BF16),
            pltpu.VMEM((ratio, block, columns), BF16),
            dma((heads, heads)),
            dma((heads, heads)),
            dma((heads, group)),
            dma((heads, group)),
            dma((heads, heads, group)),
            dma((heads, heads, group)),
            dma((narrow,)),
            dma((narrow,)),
            dma((ratio,)),
            dma((ratio,)),
        ],
        compiler_params=pltpu.CompilerParams(
            vmem_limit_bytes=56 * 1024 * 1024, collective_id=1, has_side_effects=True
        ),
        name="finish",
    )(attended, out_weight, routes_all)


def solution(mesh):
    placed = (
        P("wide", "narrow"),
        P(),
        P(),
        P("wide", None),
        P("narrow", "wide"),
        P("narrow", "wide"),
        P("narrow", "wide"),
        P("wide", "narrow"),
        P(),
        P(),
    )
    return jax.shard_map(
        functools.partial(on_device, mesh.shape["wide"], mesh.shape["narrow"]),
        mesh=mesh,
        in_specs=placed,
        out_specs=P("wide", "narrow"),
        check_vma=False,
    )
```

```python
import functools
import math

import jax
import jax.numpy as jnp
from jax import lax
from jax.experimental import pallas as pl
from jax.experimental.pallas import tpu as pltpu
from jax.sharding import PartitionSpec as P

H = 128
E = 8
EPS = 1e-06
FLOOR = -1e30
F32 = jnp.float32
BF16 = jnp.bfloat16
NT = (((1,), (1,)), ((), ()))
TN = (((0,), (0,)), ((), ()))


def pick(routes_column, blocks):
    found = jnp.zeros_like(blocks[0])
    for expert, block in enumerate(blocks):
        found = jnp.where(routes_column == expert, block, found)
    return found


def route_columns(routes_rows):
    turned = jnp.transpose(routes_rows)
    return turned[:, 0:1], turned[:, 1:2]


def attend_kernel(
    group, suffix_ref, prefix_ref, sub_ref, normed_ref, router_ref, query_ref, routes_ref,
    cache_ref, kv_ref, out_ref
):
    strands, block = normed_ref.shape[:2]
    for_each = functools.partial(
        attend_strand, group, strands, block, suffix_ref, prefix_ref, sub_ref, normed_ref,
        router_ref, query_ref, routes_ref, cache_ref, kv_ref, out_ref
    )
    lax.fori_loop(0, strands, lambda i, none: for_each(i), None)


def attend_strand(
    group, strands, block, suffix_ref, prefix_ref, sub_ref, normed_ref, router_ref, query_ref,
    routes_ref, cache_ref, kv_ref, out_ref, strand
):
    tenants = suffix_ref.shape[0]
    cache_rows = cache_ref.shape[0]
    cache_block = math.gcd(cache_rows, 512)
    wide, columns = query_ref.shape[0], query_ref.shape[2]
    token_block = strand * group + sub_ref[0]
    first = token_block * block
    last = first + block - 1

    normed = normed_ref[strand]
    logits = jnp.dot(normed, router_ref[...], preferred_element_type=F32)
    expert_at = lax.broadcasted_iota(jnp.int32, logits.shape, 1)
    route_a, route_b = route_columns(routes_ref[token_block])
    logit_a = jnp.sum(jnp.where(expert_at == route_a, logits, 0.0), axis=1, keepdims=True)
    logit_b = jnp.sum(jnp.where(expert_at == route_b, logits, 0.0), axis=1, keepdims=True)
    top = jnp.maximum(logit_a, logit_b)
    up_a, up_b = jnp.exp(logit_a - top), jnp.exp(logit_b - top)
    gate_a, gate_b = up_a / (up_a + up_b), up_b / (up_a + up_b)

    every = jnp.zeros((block, E * H), F32)
    for w in range(wide):
        every = every + lax.dot_general(
            normed[:, w * columns:(w + 1) * columns], query_ref[w], NT, preferred_element_type=F32
        )
    parts = [every[:, e * H:(e + 1) * H] for e in range(E)]
    queries = jnp.concatenate([pick(route_a, parts), pick(route_b, parts)], axis=0).astype(BF16)

    token = first + lax.broadcasted_iota(jnp.int32, (1, block), 1)
    low = jnp.zeros((1, block), jnp.int32)
    high = jnp.zeros((1, block), jnp.int32)
    start = jnp.zeros((1, block), jnp.int32)
    low_block = jnp.int32(0)
    high_block = jnp.int32(0)
    start_block = jnp.int32(0)
    suffix_at = jnp.int32(0)
    prefix_at = jnp.int32(0)
    for tenant in range(tenants):
        suffix_end = suffix_at + suffix_ref[tenant]
        prefix_end = prefix_at + prefix_ref[tenant]
        inside = (token >= suffix_at) & (token < suffix_end)
        low = jnp.where(inside, prefix_at, low)
        high = jnp.where(inside, prefix_end, high)
        start = jnp.where(inside, suffix_at, start)
        holds_first = (first >= suffix_at) & (first < suffix_end)
        holds_last = (last >= suffix_at) & (last < suffix_end)
        low_block = jnp.where(holds_first, prefix_at, low_block)
        start_block = jnp.where(holds_first, suffix_at, start_block)
        high_block = jnp.where(holds_last, prefix_end, high_block)
        suffix_at, prefix_at = suffix_end, prefix_end
    twice = lambda row: jnp.concatenate([row, row], axis=1)
    low, high, start, upto = twice(low), twice(high), twice(start), twice(token + 1)
    to_log2 = math.log2(math.e) * H ** (-0.5)
    rows = 2 * block

    def over(carried, keys, values, key_first, row_low, row_high):
        highest, totals, summed = carried
        scores = lax.dot_general(keys, queries, NT, preferred_element_type=F32)
        at = key_first + lax.broadcasted_iota(jnp.int32, scores.shape, 0)
        scores = jnp.where((at >= row_low) & (at < row_high), scores, -jnp.inf)
        new_highest = jnp.maximum(highest, jnp.max(scores, axis=0, keepdims=True))
        weights = jnp.exp2((scores - new_highest) * to_log2)
        factor = jnp.exp2((highest - new_highest) * to_log2)
        totals = totals * factor + jnp.sum(weights, axis=0, keepdims=True)
        summed = summed * factor + lax.dot_general(
            values, weights.astype(BF16), TN, preferred_element_type=F32
        )
        return new_highest, totals, summed

    def over_cache(step, carried):
        at = pl.multiple_of(step * cache_block, cache_block)
        here = cache_ref[pl.ds(at, cache_block), :]
        return over(carried, here[:, :H], here[:, H:], at, low, high)

    def over_suffix(step, carried):
        place = lax.rem(step, group) * strands + lax.div(step, group)
        here = kv_ref[pl.ds(pl.multiple_of(place * block, block), block), :]
        return over(carried, here[:, :H], here[:, H:], step * block, start, upto)

    carried = (
        jnp.full((1, rows), FLOOR, F32),
        jnp.zeros((1, rows), F32),
        jnp.zeros((H, rows), F32),
    )
    carried = lax.fori_loop(
        lax.div(low_block, cache_block),
        lax.div(high_block + cache_block - 1, cache_block),
        over_cache,
        carried,
    )
    carried = lax.fori_loop(lax.div(start_block, block), token_block + 1, over_suffix, carried)
    unused, totals, summed = carried
    attended = jnp.transpose(summed / totals)
    out_ref[strand, 0] = (attended[:block] * gate_a).astype(BF16)
    out_ref[strand, 1] = (attended[block:] * gate_b).astype(BF16)


def remote(source, target, send_sem, recv_sem, place):
    return pltpu.make_async_remote_copy(
        src_ref=source,
        dst_ref=target,
        send_sem=send_sem,
        recv_sem=recv_sem,
        device_id=place,
        device_id_type=pl.DeviceIdType.MESH,
    )


def greet(place):
    pl.semaphore_signal(
        pltpu.get_barrier_semaphore(),
        inc=1,
        device_id=place,
        device_id_type=pl.DeviceIdType.MESH,
    )


def prepare_kernel(
    wide, narrow, group, tokens_ref, gain_ref, routes_ref, kvw_ref, query_ref, cache_ref,
    normed_out, query_out, cache_out, kv_out, routes_out,
    held_tokens, held_kvw,
    tok_send, tok_recv, rt_send, rt_recv, first_send, first_recv, pass_send, pass_recv,
    sib_send, sib_recv, near_send, near_recv, kv_send, kv_recv, local_sem
):
    heads = wide // group
    block, features = tokens_ref.shape
    columns = kvw_ref.shape[1]
    slots = cache_ref.shape[0]
    me, depth = lax.axis_index("wide"), lax.axis_index("narrow")
    head, sub = lax.div(me, group), lax.rem(me, group)

    for k in range(1, wide):
        greet((lax.rem(me + k, wide), depth))
    for k in range(1, narrow):
        greet((me, lax.rem(depth + k, narrow)))
    pl.semaphore_wait(pltpu.get_barrier_semaphore(), wide - 1 + narrow - 1)

    def ahead(ka):
        return lax.rem(head + ka, heads)

    def behind(ka):
        return lax.rem(head + heads - ka, heads)

    def sibling(ks):
        return (head * group + lax.rem(sub + ks, group), depth)

    def sub_behind(s, ks):
        return lax.rem(s + group - ks, group)

    def source(kind, of_head, part):
        whole = (2 * H, E * H, slots)[kind]
        size = whole if part is None else whole // group
        offset = 0 if part is None else part * size
        if kind == 2:
            return cache_ref.at[
                pl.ds(pl.multiple_of(offset, 16), size),
                pl.ds(pl.multiple_of(of_head * 2 * H, 2 * H), 2 * H),
            ]
        ref = (kvw_ref, query_ref)[kind]
        return ref.at[pl.ds(pl.multiple_of(of_head * whole + offset, 16), size), :]

    def target(kind, origin, part):
        whole = (2 * H, E * H, slots)[kind]
        size = whole if part is None else whole // group
        offset = 0 if part is None else part * size
        if kind == 2:
            return cache_out.at[pl.ds(pl.multiple_of(origin * slots + offset, 16), size), :]
        ref = (held_kvw, query_out)[kind]
        return ref.at[origin, pl.ds(pl.multiple_of(offset, 16), size), :]

    def tok(k):
        return remote(
            tokens_ref, held_tokens.at[depth], tok_send.at[k], tok_recv.at[k],
            (me, lax.rem(depth + k, narrow))
        )

    def tok_in(k):
        return remote(
            tokens_ref, held_tokens.at[lax.rem(depth + narrow - k, narrow)], tok_send.at[k],
            tok_recv.at[k], (me, lax.rem(depth + k, narrow))
        )

    def rt(k):
        return remote(
            routes_ref, routes_out.at[me], rt_send.at[k], rt_recv.at[k],
            (lax.rem(me + k, wide), depth)
        )

    def rt_in(k):
        return remote(
            routes_ref, routes_out.at[lax.rem(me + wide - k, wide)], rt_send.at[k],
            rt_recv.at[k], (lax.rem(me + k, wide), depth)
        )

    def first(kind, ka, ks):
        to_sub = lax.rem(sub + ks, group)
        return remote(
            source(kind, ahead(ka), to_sub), target(kind, me, to_sub),
            first_send.at[kind, ka, ks], first_recv.at[kind, ka, ks],
            (ahead(ka) * group + to_sub, depth)
        )

    def first_in(kind, ka, ks):
        origin = behind(ka) * group + sub_behind(sub, ks)
        return remote(
            source(kind, head, sub), target(kind, origin, sub),
            first_send.at[kind, ka, ks], first_recv.at[kind, ka, ks], (origin, depth)
        )

    def hand(kind, ka, ks, js):
        held = target(kind, behind(ka) * group + sub_behind(sub, ks), sub)
        return remote(
            held, held, pass_send.at[kind, ka, ks, js], pass_recv.at[kind, ka, ks, js], sibling(js)
        )

    def hand_in(kind, ka, ks, js):
        other = sub_behind(sub, js)
        held = target(kind, behind(ka) * group + sub_behind(other, ks), other)
        return remote(
            held, held, pass_send.at[kind, ka, ks, js], pass_recv.at[kind, ka, ks, js], sibling(js)
        )

    def sib(kind, js):
        return remote(
            source(kind, head, None), target(kind, me, None), sib_send.at[kind, js],
            sib_recv.at[kind, js], sibling(js)
        )

    def sib_in(kind, js):
        return remote(
            source(kind, head, None), target(kind, head * group + sub_behind(sub, js), None),
            sib_send.at[kind, js], sib_recv.at[kind, js], sibling(js)
        )

    def local(kind):
        return pltpu.make_async_copy(
            source(kind, head, None), target(kind, me, None), local_sem.at[kind]
        )

    def launch(kind):
        for ka in range(1, heads):
            for ks in range(group):
                first(kind, ka, ks).start()
        for js in range(1, group):
            sib(kind, js).start()
        local(kind).start()

    def relay(kind):
        for ka in range(1, heads):
            for ks in range(group):
                first_in(kind, ka, ks).wait_recv()
                for js in range(1, group):
                    hand(kind, ka, ks, js).start()

    def settle(kind):
        local(kind).wait()
        for js in range(1, group):
            sib_in(kind, js).wait_recv()
            for ka in range(1, heads):
                for ks in range(group):
                    hand_in(kind, ka, ks, js).wait_recv()

    for k in range(1, narrow):
        tok(k).start()
    for k in range(1, wide):
        rt(k).start()
    launch(0)
    launch(1)
    routes_out[me] = routes_ref[...]
    held_tokens[depth] = tokens_ref[...]
    for k in range(1, narrow):
        tok_in(k).wait_recv()
    squares = jnp.zeros((block, 1), F32)
    for k in range(narrow):
        floats = held_tokens[k].astype(F32)
        squares = squares + jnp.sum(floats * floats, axis=1, keepdims=True)
    inverse = lax.rsqrt(squares / (narrow * features) + EPS)
    for k in range(narrow):
        at = slice(k * features, (k + 1) * features)
        normed_out[head, :, at] = (
            held_tokens[k].astype(F32) * inverse * gain_ref[:, at].astype(F32)
        ).astype(BF16)

    square = heads == 4
    half = block // 2
    if square:
        x, y = lax.rem(head, 2), lax.div(head, 2)
        neighbour = [y * 2 + 1 - x, (1 - y) * 2 + x]
        far = (1 - y) * 2 + 1 - x

    def near(side, piece):
        held = normed_out.at[head, pl.ds(piece * half, half), :]
        return remote(
            held, held, near_send.at[side, piece], near_recv.at[side, piece],
            (neighbour[side] * group + sub, depth)
        )

    def near_in(side, piece):
        held = normed_out.at[neighbour[side], pl.ds(piece * half, half), :]
        return remote(
            held, held, near_send.at[side, piece], near_recv.at[side, piece],
            (neighbour[side] * group + sub, depth)
        )

    def onward(piece):
        held = normed_out.at[neighbour[piece], pl.ds(piece * half, half), :]
        return remote(
            held, held, near_send.at[2, piece], near_recv.at[2, piece],
            (neighbour[1 - piece] * group + sub, depth)
        )

    def onward_in(piece):
        held = normed_out.at[far, pl.ds(piece * half, half), :]
        return remote(
            held, held, near_send.at[2, piece], near_recv.at[2, piece],
            (neighbour[1 - piece] * group + sub, depth)
        )

    def straight(ka):
        held = normed_out.at[head]
        return remote(
            held, held, near_send.at[0, ka], near_recv.at[0, ka], (ahead(ka) * group + sub, depth)
        )

    def straight_in(ka):
        held = normed_out.at[behind(ka)]
        return remote(
            held, held, near_send.at[0, ka], near_recv.at[0, ka], (behind(ka) * group + sub, depth)
        )

    if square:
        for turn in range(2):
            for side in range(2):
                near(side, (side + turn) % 2).start()
    else:
        for ka in range(1, heads):
            straight(ka).start()
    launch(2)
    relay(0)
    settle(0)

    def keys_values(strand):
        total = jnp.zeros((block, 2 * H), F32)
        for w in range(wide):
            total = total + lax.dot_general(
                normed_out[strand, :, w * columns:(w + 1) * columns], held_kvw[w], NT,
                preferred_element_type=F32
            )
        kv_out[sub, strand] = total.astype(BF16)

    def kv_pair(k, strand, js):
        held = kv_out.at[sub, strand]
        return remote(held, held, kv_send.at[k, js], kv_recv.at[k, js], sibling(js))

    def kv_pair_in(k, strand, js):
        held = kv_out.at[sub_behind(sub, js), strand]
        return remote(held, held, kv_send.at[k, js], kv_recv.at[k, js], sibling(js))

    if square:
        order = [head, neighbour[0], neighbour[1], far]
    else:
        order = [behind(ka) for ka in range(heads)]

    def strand_done(k):
        keys_values(order[k])
        for js in range(1, group):
            kv_pair(k, order[k], js).start()

    strand_done(0)
    relay(1)
    if square:
        for piece in range(2):
            near_in(piece, piece).wait_recv()
            onward(piece).start()
        for side in range(2):
            near_in(side, 1 - side).wait_recv()
            strand_done(1 + side)
    else:
        for ka in range(1, heads):
            straight_in(ka).wait_recv()
            strand_done(ka)
    relay(2)
    if square:
        for piece in range(2):
            onward_in(piece).wait_recv()
        strand_done(3)
    settle(1)
    settle(2)
    for k in range(heads):
        for js in range(1, group):
            kv_pair_in(k, order[k], js).wait_recv()
    for k in range(1, wide):
        rt_in(k).wait_recv()

    for k in range(1, narrow):
        tok(k).wait_send()
    for k in range(1, wide):
        rt(k).wait_send()
    for kind in range(3):
        for js in range(1, group):
            sib(kind, js).wait_send()
        for ka in range(1, heads):
            for ks in range(group):
                first(kind, ka, ks).wait_send()
                for js in range(1, group):
                    hand(kind, ka, ks, js).wait_send()
    if square:
        for side in range(2):
            for piece in range(2):
                near(side, piece).wait_send()
        for piece in range(2):
            onward(piece).wait_send()
    else:
        for ka in range(1, heads):
            straight(ka).wait_send()
    for k in range(heads):
        for js in range(1, group):
            kv_pair(k, order[k], js).wait_send()


def finish_kernel(
    wide, narrow, group, attended_ref, weight_ref, routes_ref, out_ref,
    gathered, parts, got, mine, final,
    ring_send, ring_recv, pair_send, pair_recv, pass_send, pass_recv,
    deep_send, deep_recv, turn_send, turn_recv
):
    heads = wide // group
    ratio = wide // narrow
    block = attended_ref.shape[2]
    columns = weight_ref.shape[1]
    me, depth = lax.axis_index("wide"), lax.axis_index("narrow")
    head, sub = lax.div(me, group), lax.rem(me, group)
    turned = lax.div(me, ratio)
    lane = lax.rem(me, ratio)

    for k in range(1, wide):
        greet((lax.rem(me + k, wide), depth))
    for k in range(1, narrow):
        greet((me, lax.rem(depth + k, narrow)))
    for u in range(ratio):
        @pl.when(jnp.logical_or(ratio * depth + u != me, turned != depth))
        def _():
            greet((ratio * depth + u, turned))
    own_turn = (turned == depth).astype(jnp.int32)
    pl.semaphore_wait(pltpu.get_barrier_semaphore(), wide - 1 + narrow - 1 + ratio - own_turn)

    strand_at = [lax.rem(depth + 1 + k, heads) for k in range(heads)]
    sibling = [head * group + lax.rem(sub + ks, group) for ks in range(group)]

    def ring(k, ka):
        i = strand_at[k]
        other = lax.rem(head + ka, heads) * group + sub
        return remote(
            attended_ref.at[i], gathered.at[head, sub, i],
            ring_send.at[k, ka], ring_recv.at[k, ka], (other, depth)
        )

    def ring_in(k, ka):
        i = strand_at[k]
        source = lax.rem(head + heads - ka, heads)
        return remote(
            attended_ref.at[i], gathered.at[source, sub, i],
            ring_send.at[k, ka], ring_recv.at[k, ka], (source * group + sub, depth)
        )

    def pair(k, ks):
        i = strand_at[k]
        return remote(
            attended_ref.at[i], gathered.at[head, sub, i],
            pair_send.at[k, ks], pair_recv.at[k, ks], (sibling[ks], depth)
        )

    def pair_in(k, ks):
        i = strand_at[k]
        return remote(
            attended_ref.at[i], gathered.at[head, lax.rem(sub + group - ks, group), i],
            pair_send.at[k, ks], pair_recv.at[k, ks], (sibling[ks], depth)
        )

    def hand(k, ka, ks):
        i = strand_at[k]
        held = gathered.at[lax.rem(head + heads - ka, heads), sub, i]
        return remote(held, held, pass_send.at[k, ka, ks], pass_recv.at[k, ka, ks], (sibling[ks], depth))

    def hand_in(k, ka, ks):
        i = strand_at[k]
        held = gathered.at[
            lax.rem(head + heads - ka, heads), lax.rem(sub + group - ks, group), i
        ]
        return remote(held, held, pass_send.at[k, ka, ks], pass_recv.at[k, ka, ks], (sibling[ks], depth))

    for k in range(heads):
        for ka in range(1, heads):
            ring(k, ka).start()
        for ks in range(1, group):
            pair(k, ks).start()
    for k in range(heads):
        gathered[head, sub, strand_at[k]] = attended_ref[strand_at[k]]

    def stage(k):
        for ka in range(1, heads):
            ring_in(k, ka).wait_recv()
            for ks in range(1, group):
                hand(k, ka, ks).start()

    def arrive(k):
        for ks in range(1, group):
            pair_in(k, ks).wait_recv()
            for ka in range(1, heads):
                hand_in(k, ka, ks).wait_recv()

    def project(which):
        route_a, route_b = route_columns(routes_ref[which])
        total = jnp.zeros((block, columns), F32)
        for h in range(heads):
            first = gathered[h, lax.rem(which, group), lax.div(which, group), 0]
            second = gathered[h, lax.rem(which, group), lax.div(which, group), 1]
            nothing = jnp.zeros_like(first)
            padded = jnp.concatenate(
                [
                    jnp.where(route_a == e, first, jnp.where(route_b == e, second, nothing))
                    for e in range(E)
                ],
                axis=1,
            )
            total = total + jnp.dot(
                padded, weight_ref[h * E * H:(h + 1) * E * H, :], preferred_element_type=F32
            )
        return total

    def deep(k):
        to = lax.rem(depth + 1 + k, narrow)
        return remote(parts.at[k], got.at[k], deep_send.at[k], deep_recv.at[k], (me, to))

    one_each = narrow == heads
    if one_each:
        stage(0)
    else:
        for k in range(heads):
            stage(k)
        for k in range(heads):
            arrive(k)
    owned = []
    for k in range(narrow):
        if one_each:
            if k + 1 < heads:
                stage(k + 1)
            arrive(k)
        quarter = lax.rem(depth + 1 + k, narrow)
        for u in range(ratio):
            total = project(quarter * ratio + u)
            if k < narrow - 1:
                parts[k, u] = total.astype(BF16)
            else:
                owned.append(total)
        if k < narrow - 1:
            deep(k).start()
    for k in range(narrow - 1):
        deep(k).wait_recv()
    for u in range(ratio):
        total = owned[u]
        for k in range(narrow - 1):
            total = total + got[k, u].astype(F32)
        mine[u] = total.astype(BF16)

    def turn(u):
        return remote(
            mine.at[u], final.at[lane], turn_send.at[u], turn_recv.at[lane],
            (ratio * depth + u, turned)
        )

    def turn_in(u):
        return remote(
            mine.at[u], final.at[u], turn_send.at[u], turn_recv.at[u],
            (ratio * depth + u, turned)
        )

    for u in range(ratio):
        apart = jnp.logical_or(ratio * depth + u != me, turned != depth)

        @pl.when(apart)
        def _():
            turn(u).start()

        @pl.when(jnp.logical_not(apart))
        def _():
            final[lane] = mine[u]

    for u in range(ratio):
        apart = jnp.logical_or(ratio * depth + u != me, turned != depth)

        @pl.when(apart)
        def _():
            turn_in(u).wait_recv()

        out_ref[:, u * columns:(u + 1) * columns] = final[u]

    for k in range(heads):
        for ka in range(1, heads):
            ring(k, ka).wait_send()
            for ks in range(1, group):
                hand(k, ka, ks).wait_send()
        for ks in range(1, group):
            pair(k, ks).wait_send()
    for k in range(narrow - 1):
        deep(k).wait_send()
    for u in range(ratio):
        @pl.when(jnp.logical_or(ratio * depth + u != me, turned != depth))
        def _():
            turn(u).wait_send()


def on_device(
    wide,
    narrow,
    tokens,
    norm_gain,
    router,
    routes,
    kv_weight,
    query_weight,
    out_weight,
    prefix_cache,
    suffix_lengths,
    prefix_lengths,
):
    block = tokens.shape[0]
    width = router.shape[0]
    heads = kv_weight.shape[0] // (2 * H)
    group = wide // heads
    strands = wide // group
    columns = width // wide
    slots = prefix_cache.shape[0]
    sub = lax.rem(lax.axis_index("wide"), group)
    smem = pl.BlockSpec(memory_space=pltpu.SMEM)
    in_vmem = pl.BlockSpec(memory_space=pltpu.VMEM)
    anywhere = pl.BlockSpec(memory_space=pl.ANY)
    dma = pltpu.SemaphoreType.DMA
    normed, query_rows, cache, kv, routes_all = pl.pallas_call(
        functools.partial(prepare_kernel, wide, narrow, group),
        out_shape=[
            jax.ShapeDtypeStruct((strands, block, width), BF16),
            jax.ShapeDtypeStruct((wide, E * H, columns), BF16),
            jax.ShapeDtypeStruct((wide * slots, 2 * H), BF16),
            jax.ShapeDtypeStruct((group, strands, block, 2 * H), BF16),
            jax.ShapeDtypeStruct((wide, 8, block), jnp.int32),
        ],
        in_specs=[in_vmem] * 3 + [anywhere] * 3,
        out_specs=[in_vmem] * 5,
        scratch_shapes=[
            pltpu.VMEM((narrow,) + tokens.shape, BF16),
            pltpu.VMEM((wide, 2 * H, columns), BF16),
            dma((narrow,)),
            dma((narrow,)),
            dma((wide,)),
            dma((wide,)),
            dma((3, heads, group)),
            dma((3, heads, group)),
            dma((3, heads, group, group)),
            dma((3, heads, group, group)),
            dma((3, group)),
            dma((3, group)),
            dma((3, max(2, heads))),
            dma((3, max(2, heads))),
            dma((heads, group)),
            dma((heads, group)),
            dma((3,)),
        ],
        compiler_params=pltpu.CompilerParams(
            vmem_limit_bytes=56 * 1024 * 1024, collective_id=2, has_side_effects=True
        ),
        name="prepare",
    )(
        tokens,
        norm_gain[None, :],
        jnp.pad(jnp.transpose(routes), ((0, 6), (0, 0))),
        kv_weight,
        query_weight,
        prefix_cache,
    )
    attended = pl.pallas_call(
        functools.partial(attend_kernel, group),
        out_shape=jax.ShapeDtypeStruct((strands, 2, block, H), BF16),
        in_specs=[smem] * 3 + [in_vmem] * 6,
        out_specs=in_vmem,
        compiler_params=pltpu.CompilerParams(vmem_limit_bytes=56 * 1024 * 1024),
        name="attend",
    )(
        suffix_lengths,
        prefix_lengths,
        sub[None],
        normed,
        router,
        query_rows,
        routes_all,
        cache,
        kv.reshape(wide * block, 2 * H),
    )
    ratio = wide // narrow
    return pl.pallas_call(
        functools.partial(finish_kernel, wide, narrow, group),
        out_shape=jax.ShapeDtypeStruct((block, ratio * columns), BF16),
        in_specs=[in_vmem] * 3,
        out_specs=in_vmem,
        scratch_shapes=[
            pltpu.VMEM((heads, group, strands, 2, block, H), BF16),
            pltpu.VMEM((narrow - 1, ratio, block, columns), BF16),
            pltpu.VMEM((narrow - 1, ratio, block, columns), BF16),
            pltpu.VMEM((ratio, block, columns), BF16),
            pltpu.VMEM((ratio, block, columns), BF16),
            dma((heads, heads)),
            dma((heads, heads)),
            dma((heads, group)),
            dma((heads, group)),
            dma((heads, heads, group)),
            dma((heads, heads, group)),
            dma((narrow,)),
            dma((narrow,)),
            dma((ratio,)),
            dma((ratio,)),
        ],
        compiler_params=pltpu.CompilerParams(
            vmem_limit_bytes=56 * 1024 * 1024, collective_id=1, has_side_effects=True
        ),
        name="finish",
    )(attended, out_weight, routes_all)


def solution(mesh):
    placed = (
        P("wide", "narrow"),
        P(),
        P(),
        P("wide", None),
        P("narrow", "wide"),
        P("narrow", "wide"),
        P("narrow", "wide"),
        P("wide", "narrow"),
        P(),
        P(),
    )
    return jax.shard_map(
        functools.partial(on_device, mesh.shape["wide"], mesh.shape["narrow"]),
        mesh=mesh,
        in_specs=placed,
        out_specs=P("wide", "narrow"),
        check_vma=False,
    )
```

```python
import functools
import math

import jax
import jax.numpy as jnp
from jax import lax
from jax.experimental import pallas as pl
from jax.experimental.pallas import tpu as pltpu
from jax.sharding import PartitionSpec as P

H = 128
E = 8
EPS = 1e-06
FLOOR = -1e30
F32 = jnp.float32
BF16 = jnp.bfloat16
NT = (((1,), (1,)), ((), ()))
TN = (((0,), (0,)), ((), ()))


def pick(routes_column, blocks):
    found = jnp.zeros_like(blocks[0])
    for expert, block in enumerate(blocks):
        found = jnp.where(routes_column == expert, block, found)
    return found


def route_columns(routes_rows):
    turned = jnp.transpose(routes_rows)
    return turned[:, 0:1], turned[:, 1:2]


def attend_kernel(
    group, suffix_ref, prefix_ref, sub_ref, queries_ref, gates_ref, cache_ref, kv_ref, out_ref
):
    strands, rows = queries_ref.shape[:2]
    for_each = functools.partial(
        attend_strand, group, strands, rows // 2, suffix_ref, prefix_ref, sub_ref, queries_ref,
        gates_ref, cache_ref, kv_ref, out_ref
    )
    lax.fori_loop(0, strands, lambda i, none: for_each(i), None)


def attend_strand(
    group, strands, block, suffix_ref, prefix_ref, sub_ref, queries_ref, gates_ref, cache_ref,
    kv_ref, out_ref, strand
):
    tenants = suffix_ref.shape[0]
    cache_block = math.gcd(cache_ref.shape[0], 512)
    token_block = strand * group + sub_ref[0]
    first = token_block * block
    last = first + block - 1
    queries = queries_ref[strand]

    token = first + lax.broadcasted_iota(jnp.int32, (1, block), 1)
    low = jnp.zeros((1, block), jnp.int32)
    high = jnp.zeros((1, block), jnp.int32)
    start = jnp.zeros((1, block), jnp.int32)
    low_first = high_first = start_first = jnp.int32(0)
    low_last = high_last = start_last = jnp.int32(0)
    suffix_at = prefix_at = jnp.int32(0)
    for tenant in range(tenants):
        suffix_end = suffix_at + suffix_ref[tenant]
        prefix_end = prefix_at + prefix_ref[tenant]
        inside = (token >= suffix_at) & (token < suffix_end)
        low = jnp.where(inside, prefix_at, low)
        high = jnp.where(inside, prefix_end, high)
        start = jnp.where(inside, suffix_at, start)
        holds_first = (first >= suffix_at) & (first < suffix_end)
        holds_last = (last >= suffix_at) & (last < suffix_end)
        low_first = jnp.where(holds_first, prefix_at, low_first)
        high_first = jnp.where(holds_first, prefix_end, high_first)
        start_first = jnp.where(holds_first, suffix_at, start_first)
        low_last = jnp.where(holds_last, prefix_at, low_last)
        high_last = jnp.where(holds_last, prefix_end, high_last)
        start_last = jnp.where(holds_last, suffix_at, start_last)
        suffix_at, prefix_at = suffix_end, prefix_end
    twice = lambda row: jnp.concatenate([row, row], axis=1)
    low, high, start, upto = twice(low), twice(high), twice(start), twice(token + 1)
    to_log2 = math.log2(math.e) * H ** (-0.5)
    rows = 2 * block

    def over(carried, here, limits):
        highest, totals, summed = carried
        scores = lax.dot_general(here[:, :H], queries, NT, preferred_element_type=F32)
        if limits is not None:
            key_first, row_low, row_high = limits
            at = lax.broadcasted_iota(jnp.int32, scores.shape, 0)
            scores = jnp.where(
                (at >= row_low - key_first) & (at < row_high - key_first), scores, -jnp.inf
            )
        new_highest = jnp.maximum(highest, jnp.max(scores, axis=0, keepdims=True))
        weights = jnp.exp2((scores - new_highest) * to_log2)
        factor = jnp.exp2((highest - new_highest) * to_log2)
        totals = totals * factor + jnp.sum(weights, axis=0, keepdims=True)
        summed = summed * factor + lax.dot_general(
            here[:, H:], weights.astype(BF16), TN, preferred_element_type=F32
        )
        return new_highest, totals, summed

    def cache_at(step):
        return cache_ref[pl.ds(pl.multiple_of(step * cache_block, cache_block), cache_block), :]

    def suffix_at_step(step):
        place = lax.rem(step, group) * strands + lax.div(step, group)
        return kv_ref[pl.ds(pl.multiple_of(place * block, block), block), :]

    def through(carried, begin, inner_begin, inner_end, end, load, limits_at):
        inner_begin = jnp.minimum(inner_begin, end)
        inner_end = jnp.maximum(inner_end, inner_begin)
        left = inner_begin - begin

        def masked(turn, carried):
            step = begin + turn + jnp.where(turn < left, 0, inner_end - inner_begin)
            return over(carried, load(step), limits_at(step))

        carried = lax.fori_loop(0, end - begin - (inner_end - inner_begin), masked, carried)
        return lax.fori_loop(
            inner_begin, inner_end, lambda step, now: over(now, load(step), None), carried
        )

    carried = (
        jnp.full((1, rows), FLOOR, F32),
        jnp.zeros((1, rows), F32),
        jnp.zeros((H, rows), F32),
    )
    carried = through(
        carried,
        lax.div(low_first, cache_block),
        lax.div(low_last + cache_block - 1, cache_block),
        lax.div(high_first, cache_block),
        lax.div(high_last + cache_block - 1, cache_block),
        cache_at,
        lambda step: (step * cache_block, low, high),
    )
    carried = through(
        carried,
        lax.div(start_first, block),
        lax.div(start_last + block - 1, block),
        token_block,
        token_block + 1,
        suffix_at_step,
        lambda step: (step * block, start, upto),
    )
    unused, totals, summed = carried
    attended = jnp.transpose(summed / totals) * gates_ref[strand]
    out_ref[strand, 0] = attended[:block].astype(BF16)
    out_ref[strand, 1] = attended[block:].astype(BF16)


def remote(source, target, send_sem, recv_sem, place):
    return pltpu.make_async_remote_copy(
        src_ref=source,
        dst_ref=target,
        send_sem=send_sem,
        recv_sem=recv_sem,
        device_id=place,
        device_id_type=pl.DeviceIdType.MESH,
    )


def greet(place):
    pl.semaphore_signal(
        pltpu.get_barrier_semaphore(),
        inc=1,
        device_id=place,
        device_id_type=pl.DeviceIdType.MESH,
    )


def prepare_kernel(
    wide, narrow, group, tokens_ref, gain_ref, routes_ref, router_ref, kvw_ref, query_ref,
    cache_ref, queries_out, gates_out, cache_out, kv_out, routes_out,
    held_tokens, normed_out, held_kvw, held_query, held_routes,
    tok_send, tok_recv, rt_send, rt_recv, first_send, first_recv, pass_send, pass_recv,
    sib_send, sib_recv, near_send, near_recv, kv_send, kv_recv, local_sem
):
    heads = wide // group
    block, features = tokens_ref.shape
    columns = kvw_ref.shape[1]
    slots = cache_ref.shape[0]
    me, depth = lax.axis_index("wide"), lax.axis_index("narrow")
    head, sub = lax.div(me, group), lax.rem(me, group)

    for k in range(1, wide):
        greet((lax.rem(me + k, wide), depth))
    for k in range(1, narrow):
        greet((me, lax.rem(depth + k, narrow)))
    pl.semaphore_wait(pltpu.get_barrier_semaphore(), wide - 1 + narrow - 1)

    def ahead(ka):
        return lax.rem(head + ka, heads)

    def behind(ka):
        return lax.rem(head + heads - ka, heads)

    def sibling(ks):
        return (head * group + lax.rem(sub + ks, group), depth)

    def sub_behind(s, ks):
        return lax.rem(s + group - ks, group)

    def source(kind, of_head, part):
        whole = (2 * H, E * H, slots)[kind]
        size = whole if part is None else whole // group
        offset = 0 if part is None else part * size
        if kind == 2:
            return cache_ref.at[
                pl.ds(pl.multiple_of(offset, 16), size),
                pl.ds(pl.multiple_of(of_head * 2 * H, 2 * H), 2 * H),
            ]
        ref = (kvw_ref, query_ref)[kind]
        return ref.at[pl.ds(pl.multiple_of(of_head * whole + offset, 16), size), :]

    def target(kind, origin, part):
        whole = (2 * H, E * H, slots)[kind]
        size = whole if part is None else whole // group
        offset = 0 if part is None else part * size
        if kind == 2:
            return cache_out.at[pl.ds(pl.multiple_of(origin * slots + offset, 16), size), :]
        ref = (held_kvw, held_query)[kind]
        return ref.at[
            pl.ds(pl.multiple_of(offset, 16), size),
            pl.ds(pl.multiple_of(origin * columns, columns), columns),
        ]

    def tok(k):
        return remote(
            tokens_ref, held_tokens.at[depth], tok_send.at[k], tok_recv.at[k],
            (me, lax.rem(depth + k, narrow))
        )

    def tok_in(k):
        return remote(
            tokens_ref, held_tokens.at[lax.rem(depth + narrow - k, narrow)], tok_send.at[k],
            tok_recv.at[k], (me, lax.rem(depth + k, narrow))
        )

    def rt(k):
        return remote(
            held_routes, routes_out.at[me], rt_send.at[k], rt_recv.at[k],
            (lax.rem(me + k, wide), depth)
        )

    def rt_in(k):
        return remote(
            held_routes, routes_out.at[lax.rem(me + wide - k, wide)], rt_send.at[k],
            rt_recv.at[k], (lax.rem(me + k, wide), depth)
        )

    def first(kind, ka, ks):
        to_sub = lax.rem(sub + ks, group)
        return remote(
            source(kind, ahead(ka), to_sub), target(kind, me, to_sub),
            first_send.at[kind, ka, ks], first_recv.at[kind, ka, ks],
            (ahead(ka) * group + to_sub, depth)
        )

    def first_in(kind, ka, ks):
        origin = behind(ka) * group + sub_behind(sub, ks)
        return remote(
            source(kind, head, sub), target(kind, origin, sub),
            first_send.at[kind, ka, ks], first_recv.at[kind, ka, ks], (origin, depth)
        )

    def hand(kind, ka, ks, js):
        held = target(kind, behind(ka) * group + sub_behind(sub, ks), sub)
        return remote(
            held, held, pass_send.at[kind, ka, ks, js], pass_recv.at[kind, ka, ks, js], sibling(js)
        )

    def hand_in(kind, ka, ks, js):
        other = sub_behind(sub, js)
        held = target(kind, behind(ka) * group + sub_behind(other, ks), other)
        return remote(
            held, held, pass_send.at[kind, ka, ks, js], pass_recv.at[kind, ka, ks, js], sibling(js)
        )

    def sib(kind, js):
        return remote(
            source(kind, head, None), target(kind, me, None), sib_send.at[kind, js],
            sib_recv.at[kind, js], sibling(js)
        )

    def sib_in(kind, js):
        return remote(
            source(kind, head, None), target(kind, head * group + sub_behind(sub, js), None),
            sib_send.at[kind, js], sib_recv.at[kind, js], sibling(js)
        )

    def local(kind):
        return pltpu.make_async_copy(
            source(kind, head, None), target(kind, me, None), local_sem.at[kind]
        )

    def launch(kind):
        for ka in range(1, heads):
            for ks in range(group):
                first(kind, ka, ks).start()
        for js in range(1, group):
            sib(kind, js).start()
        local(kind).start()

    def relay(kind):
        for ka in range(1, heads):
            for ks in range(group):
                first_in(kind, ka, ks).wait_recv()
                for js in range(1, group):
                    hand(kind, ka, ks, js).start()

    def settle(kind):
        local(kind).wait()
        for js in range(1, group):
            sib_in(kind, js).wait_recv()
            for ka in range(1, heads):
                for ks in range(group):
                    hand_in(kind, ka, ks, js).wait_recv()

    for k in range(1, narrow):
        tok(k).start()
    held_routes[...] = jnp.zeros_like(held_routes)
    held_routes[0:2, :] = routes_ref[...]
    for k in range(1, wide):
        rt(k).start()
    launch(0)
    launch(1)
    routes_out[me] = held_routes[...]
    held_tokens[depth] = tokens_ref[...]
    for k in range(1, narrow):
        tok_in(k).wait_recv()
    squares = jnp.zeros((block, 1), F32)
    for k in range(narrow):
        floats = held_tokens[k].astype(F32)
        squares = squares + jnp.sum(floats * floats, axis=1, keepdims=True)
    inverse = lax.rsqrt(squares / (narrow * features) + EPS)
    for k in range(narrow):
        at = slice(k * features, (k + 1) * features)
        normed_out[head, :, at] = (
            held_tokens[k].astype(F32) * inverse * gain_ref[at].astype(F32)[None, :]
        ).astype(BF16)

    square = heads == 4
    half = block // 2
    if square:
        x, y = lax.rem(head, 2), lax.div(head, 2)
        neighbour = [y * 2 + 1 - x, (1 - y) * 2 + x]
        far = (1 - y) * 2 + 1 - x

    def near(side, piece):
        held = normed_out.at[head, pl.ds(piece * half, half), :]
        return remote(
            held, held, near_send.at[side, piece], near_recv.at[side, piece],
            (neighbour[side] * group + sub, depth)
        )

    def near_in(side, piece):
        held = normed_out.at[neighbour[side], pl.ds(piece * half, half), :]
        return remote(
            held, held, near_send.at[side, piece], near_recv.at[side, piece],
            (neighbour[side] * group + sub, depth)
        )

    def onward(piece):
        held = normed_out.at[neighbour[piece], pl.ds(piece * half, half), :]
        return remote(
            held, held, near_send.at[2, piece], near_recv.at[2, piece],
            (neighbour[1 - piece] * group + sub, depth)
        )

    def onward_in(piece):
        held = normed_out.at[far, pl.ds(piece * half, half), :]
        return remote(
            held, held, near_send.at[2, piece], near_recv.at[2, piece],
            (neighbour[1 - piece] * group + sub, depth)
        )

    def straight(ka):
        held = normed_out.at[head]
        return remote(
            held, held, near_send.at[0, ka], near_recv.at[0, ka], (ahead(ka) * group + sub, depth)
        )

    def straight_in(ka):
        held = normed_out.at[behind(ka)]
        return remote(
            held, held, near_send.at[0, ka], near_recv.at[0, ka], (behind(ka) * group + sub, depth)
        )

    if square:
        for turn in range(2):
            for side in range(2):
                near(side, (side + turn) % 2).start()
    else:
        for ka in range(1, heads):
            straight(ka).start()
    launch(2)
    relay(0)
    settle(0)

    def keys_values(strand):
        total = lax.dot_general(
            normed_out[strand], held_kvw[...], NT, preferred_element_type=F32
        )
        kv_out[sub, strand] = total.astype(BF16)

    def queries_of(strand):
        normed = normed_out[strand]
        logits = lax.dot_general(normed, router_ref[...], NT, preferred_element_type=F32)
        expert_at = lax.broadcasted_iota(jnp.int32, logits.shape, 1)
        route_a, route_b = route_columns(routes_out[strand * group + sub])
        logit_a = jnp.sum(jnp.where(expert_at == route_a, logits, 0.0), axis=1, keepdims=True)
        logit_b = jnp.sum(jnp.where(expert_at == route_b, logits, 0.0), axis=1, keepdims=True)
        top = jnp.maximum(logit_a, logit_b)
        up_a, up_b = jnp.exp(logit_a - top), jnp.exp(logit_b - top)
        gates_out[strand, :block] = up_a / (up_a + up_b)
        gates_out[strand, block:] = up_b / (up_a + up_b)
        every = lax.dot_general(normed, held_query[...], NT, preferred_element_type=F32)
        parts = [every[:, e * H:(e + 1) * H] for e in range(E)]
        queries_out[strand, :block] = pick(route_a, parts).astype(BF16)
        queries_out[strand, block:] = pick(route_b, parts).astype(BF16)

    def kv_pair(k, strand, js):
        held = kv_out.at[sub, strand]
        return remote(held, held, kv_send.at[k, js], kv_recv.at[k, js], sibling(js))

    def kv_pair_in(k, strand, js):
        held = kv_out.at[sub_behind(sub, js), strand]
        return remote(held, held, kv_send.at[k, js], kv_recv.at[k, js], sibling(js))

    if square:
        order = [head, neighbour[0], neighbour[1], far]
    else:
        order = [behind(ka) for ka in range(heads)]

    def strand_done(k):
        keys_values(order[k])
        for js in range(1, group):
            kv_pair(k, order[k], js).start()

    strand_done(0)
    relay(1)
    if square:
        for piece in range(2):
            near_in(piece, piece).wait_recv()
            onward(piece).start()
        for side in range(2):
            near_in(side, 1 - side).wait_recv()
            strand_done(1 + side)
    else:
        for ka in range(1, heads):
            straight_in(ka).wait_recv()
            strand_done(ka)
    settle(1)
    for k in range(1, wide):
        rt_in(k).wait_recv()
    if square:
        def early(k, none):
            queries_of(jnp.where(k == 0, head, jnp.where(k == 1, neighbour[0], neighbour[1])))

        lax.fori_loop(0, 3, early, None)
    else:
        lax.fori_loop(0, heads, lambda k, none: queries_of(k), None)
    relay(2)
    if square:
        for piece in range(2):
            onward_in(piece).wait_recv()
        strand_done(3)
        queries_of(far)
    settle(2)
    for k in range(heads):
        for js in range(1, group):
            kv_pair_in(k, order[k], js).wait_recv()

    for k in range(1, narrow):
        tok(k).wait_send()
    for k in range(1, wide):
        rt(k).wait_send()
    for kind in range(3):
        for js in range(1, group):
            sib(kind, js).wait_send()
        for ka in range(1, heads):
            for ks in range(group):
                first(kind, ka, ks).wait_send()
                for js in range(1, group):
                    hand(kind, ka, ks, js).wait_send()
    if square:
        for side in range(2):
            for piece in range(2):
                near(side, piece).wait_send()
        for piece in range(2):
            onward(piece).wait_send()
    else:
        for ka in range(1, heads):
            straight(ka).wait_send()
    for k in range(heads):
        for js in range(1, group):
            kv_pair(k, order[k], js).wait_send()


def finish_kernel(
    wide, narrow, group, attended_ref, weight_ref, routes_ref, out_ref,
    gathered, parts, got, mine, final,
    ring_send, ring_recv, pair_send, pair_recv, pass_send, pass_recv,
    deep_send, deep_recv, turn_send, turn_recv
):
    heads = wide // group
    ratio = wide // narrow
    block = attended_ref.shape[2]
    columns = weight_ref.shape[1]
    me, depth = lax.axis_index("wide"), lax.axis_index("narrow")
    head, sub = lax.div(me, group), lax.rem(me, group)
    turned = lax.div(me, ratio)
    lane = lax.rem(me, ratio)

    for k in range(1, wide):
        greet((lax.rem(me + k, wide), depth))
    for k in range(1, narrow):
        greet((me, lax.rem(depth + k, narrow)))
    for u in range(ratio):
        @pl.when(jnp.logical_or(ratio * depth + u != me, turned != depth))
        def _():
            greet((ratio * depth + u, turned))
    own_turn = (turned == depth).astype(jnp.int32)
    pl.semaphore_wait(pltpu.get_barrier_semaphore(), wide - 1 + narrow - 1 + ratio - own_turn)

    strand_at = [lax.rem(depth + 1 + k, heads) for k in range(heads)]
    sibling = [head * group + lax.rem(sub + ks, group) for ks in range(group)]

    def ring(k, ka):
        i = strand_at[k]
        other = lax.rem(head + ka, heads) * group + sub
        return remote(
            attended_ref.at[i], gathered.at[head, sub, i],
            ring_send.at[k, ka], ring_recv.at[k, ka], (other, depth)
        )

    def ring_in(k, ka):
        i = strand_at[k]
        source = lax.rem(head + heads - ka, heads)
        return remote(
            attended_ref.at[i], gathered.at[source, sub, i],
            ring_send.at[k, ka], ring_recv.at[k, ka], (source * group + sub, depth)
        )

    def pair(k, ks):
        i = strand_at[k]
        return remote(
            attended_ref.at[i], gathered.at[head, sub, i],
            pair_send.at[k, ks], pair_recv.at[k, ks], (sibling[ks], depth)
        )

    def pair_in(k, ks):
        i = strand_at[k]
        return remote(
            attended_ref.at[i], gathered.at[head, lax.rem(sub + group - ks, group), i],
            pair_send.at[k, ks], pair_recv.at[k, ks], (sibling[ks], depth)
        )

    def hand(k, ka, ks):
        i = strand_at[k]
        held = gathered.at[lax.rem(head + heads - ka, heads), sub, i]
        return remote(held, held, pass_send.at[k, ka, ks], pass_recv.at[k, ka, ks], (sibling[ks], depth))

    def hand_in(k, ka, ks):
        i = strand_at[k]
        held = gathered.at[
            lax.rem(head + heads - ka, heads), lax.rem(sub + group - ks, group), i
        ]
        return remote(held, held, pass_send.at[k, ka, ks], pass_recv.at[k, ka, ks], (sibling[ks], depth))

    for k in range(heads):
        for ka in range(1, heads):
            ring(k, ka).start()
        for ks in range(1, group):
            pair(k, ks).start()
    for k in range(heads):
        gathered[head, sub, strand_at[k]] = attended_ref[strand_at[k]]

    def stage(k):
        for ka in range(1, heads):
            ring_in(k, ka).wait_recv()
            for ks in range(1, group):
                hand(k, ka, ks).start()

    def arrive(k):
        for ks in range(1, group):
            pair_in(k, ks).wait_recv()
            for ka in range(1, heads):
                hand_in(k, ka, ks).wait_recv()

    def project(which):
        route_a, route_b = route_columns(routes_ref[which])
        total = jnp.zeros((block, columns), F32)
        for h in range(heads):
            first = gathered[h, lax.rem(which, group), lax.div(which, group), 0]
            second = gathered[h, lax.rem(which, group), lax.div(which, group), 1]
            nothing = jnp.zeros_like(first)
            padded = jnp.concatenate(
                [
                    jnp.where(route_a == e, first, jnp.where(route_b == e, second, nothing))
                    for e in range(E)
                ],
                axis=1,
            )
            total = total + jnp.dot(
                padded, weight_ref[h * E * H:(h + 1) * E * H, :], preferred_element_type=F32
            )
        return total

    def deep(k):
        to = lax.rem(depth + 1 + k, narrow)
        return remote(parts.at[k], got.at[k], deep_send.at[k], deep_recv.at[k], (me, to))

    one_each = narrow == heads
    if one_each:
        stage(0)
    else:
        for k in range(heads):
            stage(k)
        for k in range(heads):
            arrive(k)
    owned = []
    for k in range(narrow):
        if one_each:
            if k + 1 < heads:
                stage(k + 1)
            arrive(k)
        quarter = lax.rem(depth + 1 + k, narrow)
        for u in range(ratio):
            total = project(quarter * ratio + u)
            if k < narrow - 1:
                parts[k, u] = total.astype(BF16)
            else:
                owned.append(total)
        if k < narrow - 1:
            deep(k).start()
    for k in range(narrow - 1):
        deep(k).wait_recv()
    for u in range(ratio):
        total = owned[u]
        for k in range(narrow - 1):
            total = total + got[k, u].astype(F32)
        mine[u] = total.astype(BF16)

    def turn(u):
        return remote(
            mine.at[u], final.at[lane], turn_send.at[u], turn_recv.at[lane],
            (ratio * depth + u, turned)
        )

    def turn_in(u):
        return remote(
            mine.at[u], final.at[u], turn_send.at[u], turn_recv.at[u],
            (ratio * depth + u, turned)
        )

    for u in range(ratio):
        apart = jnp.logical_or(ratio * depth + u != me, turned != depth)

        @pl.when(apart)
        def _():
            turn(u).start()

        @pl.when(jnp.logical_not(apart))
        def _():
            final[lane] = mine[u]

    for u in range(ratio):
        apart = jnp.logical_or(ratio * depth + u != me, turned != depth)

        @pl.when(apart)
        def _():
            turn_in(u).wait_recv()

        out_ref[:, u * columns:(u + 1) * columns] = final[u]

    for k in range(heads):
        for ka in range(1, heads):
            ring(k, ka).wait_send()
            for ks in range(1, group):
                hand(k, ka, ks).wait_send()
        for ks in range(1, group):
            pair(k, ks).wait_send()
    for k in range(narrow - 1):
        deep(k).wait_send()
    for u in range(ratio):
        @pl.when(jnp.logical_or(ratio * depth + u != me, turned != depth))
        def _():
            turn(u).wait_send()


def on_device(
    wide,
    narrow,
    tokens,
    norm_gain,
    router,
    routes,
    kv_weight,
    query_weight,
    out_weight,
    prefix_cache,
    suffix_lengths,
    prefix_lengths,
):
    block = tokens.shape[0]
    width = router.shape[0]
    heads = kv_weight.shape[0] // (2 * H)
    group = wide // heads
    strands = wide // group
    columns = width // wide
    slots = prefix_cache.shape[0]
    sub = lax.rem(lax.axis_index("wide"), group)
    smem = pl.BlockSpec(memory_space=pltpu.SMEM)
    in_vmem = pl.BlockSpec(memory_space=pltpu.VMEM)
    anywhere = pl.BlockSpec(memory_space=pl.ANY)
    dma = pltpu.SemaphoreType.DMA
    queries, gates, cache, kv, routes_all = pl.pallas_call(
        functools.partial(prepare_kernel, wide, narrow, group),
        out_shape=[
            jax.ShapeDtypeStruct((strands, 2 * block, H), BF16),
            jax.ShapeDtypeStruct((strands, 2 * block, 1), F32),
            jax.ShapeDtypeStruct((wide * slots, 2 * H), BF16),
            jax.ShapeDtypeStruct((group, strands, block, 2 * H), BF16),
            jax.ShapeDtypeStruct((wide, 8, block), jnp.int32),
        ],
        in_specs=[in_vmem] * 4 + [anywhere] * 3,
        out_specs=[in_vmem] * 5,
        scratch_shapes=[
            pltpu.VMEM((narrow,) + tokens.shape, BF16),
            pltpu.VMEM((strands, block, width), BF16),
            pltpu.VMEM((2 * H, width), BF16),
            pltpu.VMEM((E * H, width), BF16),
            pltpu.VMEM((8, block), jnp.int32),
            dma((narrow,)),
            dma((narrow,)),
            dma((wide,)),
            dma((wide,)),
            dma((3, heads, group)),
            dma((3, heads, group)),
            dma((3, heads, group, group)),
            dma((3, heads, group, group)),
            dma((3, group)),
            dma((3, group)),
            dma((3, max(2, heads))),
            dma((3, max(2, heads))),
            dma((heads, group)),
            dma((heads, group)),
            dma((3,)),
        ],
        compiler_params=pltpu.CompilerParams(
            vmem_limit_bytes=56 * 1024 * 1024, collective_id=2, has_side_effects=True
        ),
        name="prepare",
    )(
        tokens,
        norm_gain,
        jnp.transpose(routes),
        jnp.transpose(router),
        kv_weight,
        query_weight,
        prefix_cache,
    )
    attended = pl.pallas_call(
        functools.partial(attend_kernel, group),
        out_shape=jax.ShapeDtypeStruct((strands, 2, block, H), BF16),
        in_specs=[smem] * 3 + [in_vmem] * 4,
        out_specs=in_vmem,
        compiler_params=pltpu.CompilerParams(vmem_limit_bytes=56 * 1024 * 1024),
        name="attend",
    )(
        suffix_lengths,
        prefix_lengths,
        sub[None],
        queries,
        gates,
        cache,
        kv.reshape(wide * block, 2 * H),
    )
    ratio = wide // narrow
    return pl.pallas_call(
        functools.partial(finish_kernel, wide, narrow, group),
        out_shape=jax.ShapeDtypeStruct((block, ratio * columns), BF16),
        in_specs=[in_vmem] * 3,
        out_specs=in_vmem,
        scratch_shapes=[
            pltpu.VMEM((heads, group, strands, 2, block, H), BF16),
            pltpu.VMEM((narrow - 1, ratio, block, columns), BF16),
            pltpu.VMEM((narrow - 1, ratio, block, columns), BF16),
            pltpu.VMEM((ratio, block, columns), BF16),
            pltpu.VMEM((ratio, block, columns), BF16),
            dma((heads, heads)),
            dma((heads, heads)),
            dma((heads, group)),
            dma((heads, group)),
            dma((heads, heads, group)),
            dma((heads, heads, group)),
            dma((narrow,)),
            dma((narrow,)),
            dma((ratio,)),
            dma((ratio,)),
        ],
        compiler_params=pltpu.CompilerParams(
            vmem_limit_bytes=56 * 1024 * 1024, collective_id=1, has_side_effects=True
        ),
        name="finish",
    )(attended, out_weight, routes_all)


def solution(mesh):
    placed = (
        P("wide", "narrow"),
        P(),
        P(),
        P("wide", None),
        P("narrow", "wide"),
        P("narrow", "wide"),
        P("narrow", "wide"),
        P("wide", "narrow"),
        P(),
        P(),
    )
    return jax.shard_map(
        functools.partial(on_device, mesh.shape["wide"], mesh.shape["narrow"]),
        mesh=mesh,
        in_specs=placed,
        out_specs=P("wide", "narrow"),
        check_vma=False,
    )
```

```python
import functools
import math

import jax
import jax.numpy as jnp
from jax import lax
from jax.experimental import pallas as pl
from jax.experimental.pallas import tpu as pltpu
from jax.sharding import PartitionSpec as P

H = 128
E = 8
EPS = 1e-06
FLOOR = -1e30
F32 = jnp.float32
BF16 = jnp.bfloat16
NT = (((1,), (1,)), ((), ()))
TN = (((0,), (0,)), ((), ()))


def pick(routes_column, blocks):
    found = jnp.zeros_like(blocks[0])
    for expert, block in enumerate(blocks):
        found = jnp.where(routes_column == expert, block, found)
    return found


def route_columns(routes_rows):
    turned = jnp.transpose(routes_rows)
    return turned[:, 0:1], turned[:, 1:2]


def attend_kernel(
    group, suffix_ref, prefix_ref, sub_ref, queries_ref, gates_ref, cache_ref, kv_ref, out_ref
):
    strands, rows = queries_ref.shape[:2]
    for_each = functools.partial(
        attend_strand, group, strands, rows // 2, suffix_ref, prefix_ref, sub_ref, queries_ref,
        gates_ref, cache_ref, kv_ref, out_ref
    )
    lax.fori_loop(0, strands, lambda i, none: for_each(i), None)


def attend_strand(
    group, strands, block, suffix_ref, prefix_ref, sub_ref, queries_ref, gates_ref, cache_ref,
    kv_ref, out_ref, strand
):
    tenants = suffix_ref.shape[0]
    cache_block = math.gcd(cache_ref.shape[0], 512)
    token_block = strand * group + sub_ref[0]
    first = token_block * block
    last = first + block - 1
    queries = queries_ref[strand]

    token = first + lax.broadcasted_iota(jnp.int32, (1, block), 1)
    low = jnp.zeros((1, block), jnp.int32)
    high = jnp.zeros((1, block), jnp.int32)
    start = jnp.zeros((1, block), jnp.int32)
    low_first = high_first = start_first = jnp.int32(0)
    low_last = high_last = start_last = jnp.int32(0)
    suffix_at = prefix_at = jnp.int32(0)
    for tenant in range(tenants):
        suffix_end = suffix_at + suffix_ref[tenant]
        prefix_end = prefix_at + prefix_ref[tenant]
        inside = (token >= suffix_at) & (token < suffix_end)
        low = jnp.where(inside, prefix_at, low)
        high = jnp.where(inside, prefix_end, high)
        start = jnp.where(inside, suffix_at, start)
        holds_first = (first >= suffix_at) & (first < suffix_end)
        holds_last = (last >= suffix_at) & (last < suffix_end)
        low_first = jnp.where(holds_first, prefix_at, low_first)
        high_first = jnp.where(holds_first, prefix_end, high_first)
        start_first = jnp.where(holds_first, suffix_at, start_first)
        low_last = jnp.where(holds_last, prefix_at, low_last)
        high_last = jnp.where(holds_last, prefix_end, high_last)
        start_last = jnp.where(holds_last, suffix_at, start_last)
        suffix_at, prefix_at = suffix_end, prefix_end
    twice = lambda row: jnp.concatenate([row, row], axis=1)
    low, high, start, upto = twice(low), twice(high), twice(start), twice(token + 1)
    to_log2 = math.log2(math.e) * H ** (-0.5)
    rows = 2 * block

    def over(carried, here, limits):
        highest, totals, summed = carried
        scores = lax.dot_general(here[:, :H], queries, NT, preferred_element_type=F32)
        if limits is not None:
            key_first, row_low, row_high = limits
            at = lax.broadcasted_iota(jnp.int32, scores.shape, 0)
            scores = jnp.where(
                (at >= row_low - key_first) & (at < row_high - key_first), scores, -jnp.inf
            )
        new_highest = jnp.maximum(highest, jnp.max(scores, axis=0, keepdims=True))
        weights = jnp.exp2((scores - new_highest) * to_log2)
        factor = jnp.exp2((highest - new_highest) * to_log2)
        totals = totals * factor + jnp.sum(weights, axis=0, keepdims=True)
        summed = summed * factor + lax.dot_general(
            here[:, H:], weights.astype(BF16), TN, preferred_element_type=F32
        )
        return new_highest, totals, summed

    def cache_at(step):
        return cache_ref[pl.ds(pl.multiple_of(step * cache_block, cache_block), cache_block), :]

    def suffix_at_step(step):
        place = lax.rem(step, group) * strands + lax.div(step, group)
        return kv_ref[pl.ds(pl.multiple_of(place * block, block), block), :]

    def through(carried, begin, inner_begin, inner_end, end, load, limits_at):
        inner_begin = jnp.minimum(inner_begin, end)
        inner_end = jnp.maximum(inner_end, inner_begin)
        left = inner_begin - begin

        def masked(turn, carried):
            step = begin + turn + jnp.where(turn < left, 0, inner_end - inner_begin)
            return over(carried, load(step), limits_at(step))

        carried = lax.fori_loop(0, end - begin - (inner_end - inner_begin), masked, carried)
        return lax.fori_loop(
            inner_begin, inner_end, lambda step, now: over(now, load(step), None), carried
        )

    carried = (
        jnp.full((1, rows), FLOOR, F32),
        jnp.zeros((1, rows), F32),
        jnp.zeros((H, rows), F32),
    )
    carried = through(
        carried,
        lax.div(low_first, cache_block),
        lax.div(low_last + cache_block - 1, cache_block),
        lax.div(high_first, cache_block),
        lax.div(high_last + cache_block - 1, cache_block),
        cache_at,
        lambda step: (step * cache_block, low, high),
    )
    carried = through(
        carried,
        lax.div(start_first, block),
        lax.div(start_last + block - 1, block),
        token_block,
        token_block + 1,
        suffix_at_step,
        lambda step: (step * block, start, upto),
    )
    unused, totals, summed = carried
    attended = jnp.transpose(summed / totals) * gates_ref[strand]
    out_ref[strand, 0] = attended[:block].astype(BF16)
    out_ref[strand, 1] = attended[block:].astype(BF16)


def remote(source, target, send_sem, recv_sem, place):
    return pltpu.make_async_remote_copy(
        src_ref=source,
        dst_ref=target,
        send_sem=send_sem,
        recv_sem=recv_sem,
        device_id=place,
        device_id_type=pl.DeviceIdType.MESH,
    )


def greet(place):
    pl.semaphore_signal(
        pltpu.get_barrier_semaphore(),
        inc=1,
        device_id=place,
        device_id_type=pl.DeviceIdType.MESH,
    )


def prepare_kernel(
    wide, narrow, group, tokens_ref, gain_ref, routes_ref, router_ref, kvw_ref, query_ref,
    cache_ref, queries_out, gates_out, cache_out, kv_out, routes_out,
    held_tokens, normed_out, held_kvw, held_query, held_routes,
    tok_send, tok_recv, rt_send, rt_recv, first_send, first_recv, pass_send, pass_recv,
    sib_send, sib_recv, near_send, near_recv, kv_send, kv_recv, local_sem
):
    heads = wide // group
    block, features = tokens_ref.shape
    columns = kvw_ref.shape[1]
    slots = cache_ref.shape[0]
    me, depth = lax.axis_index("wide"), lax.axis_index("narrow")
    head, sub = lax.div(me, group), lax.rem(me, group)

    for k in range(1, wide):
        greet((lax.rem(me + k, wide), depth))
    for k in range(1, narrow):
        greet((me, lax.rem(depth + k, narrow)))
    pl.semaphore_wait(pltpu.get_barrier_semaphore(), wide - 1 + narrow - 1)

    def ahead(ka):
        return lax.rem(head + ka, heads)

    def behind(ka):
        return lax.rem(head + heads - ka, heads)

    def sibling(ks):
        return (head * group + lax.rem(sub + ks, group), depth)

    def sub_behind(s, ks):
        return lax.rem(s + group - ks, group)

    def source(kind, of_head, part):
        whole = (2 * H, E * H, slots)[kind]
        size = whole if part is None else whole // group
        offset = 0 if part is None else part * size
        if kind == 2:
            return cache_ref.at[
                pl.ds(pl.multiple_of(offset, 16), size),
                pl.ds(pl.multiple_of(of_head * 2 * H, 2 * H), 2 * H),
            ]
        ref = (kvw_ref, query_ref)[kind]
        return ref.at[pl.ds(pl.multiple_of(of_head * whole + offset, 16), size), :]

    def target(kind, origin, part):
        whole = (2 * H, E * H, slots)[kind]
        size = whole if part is None else whole // group
        offset = 0 if part is None else part * size
        if kind == 2:
            return cache_out.at[pl.ds(pl.multiple_of(origin * slots + offset, 16), size), :]
        ref = (held_kvw, held_query)[kind]
        return ref.at[
            pl.ds(pl.multiple_of(offset, 16), size),
            pl.ds(pl.multiple_of(origin * columns, columns), columns),
        ]

    def tok(k):
        return remote(
            tokens_ref, held_tokens.at[depth], tok_send.at[k], tok_recv.at[k],
            (me, lax.rem(depth + k, narrow))
        )

    def tok_in(k):
        return remote(
            tokens_ref, held_tokens.at[lax.rem(depth + narrow - k, narrow)], tok_send.at[k],
            tok_recv.at[k], (me, lax.rem(depth + k, narrow))
        )

    def rt(k):
        return remote(
            held_routes, routes_out.at[me], rt_send.at[k], rt_recv.at[k],
            (lax.rem(me + k, wide), depth)
        )

    def rt_in(k):
        return remote(
            held_routes, routes_out.at[lax.rem(me + wide - k, wide)], rt_send.at[k],
            rt_recv.at[k], (lax.rem(me + k, wide), depth)
        )

    def first(kind, ka, ks):
        to_sub = lax.rem(sub + ks, group)
        return remote(
            source(kind, ahead(ka), to_sub), target(kind, me, to_sub),
            first_send.at[kind, ka, ks], first_recv.at[kind, ka, ks],
            (ahead(ka) * group + to_sub, depth)
        )

    def first_in(kind, ka, ks):
        origin = behind(ka) * group + sub_behind(sub, ks)
        return remote(
            source(kind, head, sub), target(kind, origin, sub),
            first_send.at[kind, ka, ks], first_recv.at[kind, ka, ks], (origin, depth)
        )

    def hand(kind, ka, ks, js):
        held = target(kind, behind(ka) * group + sub_behind(sub, ks), sub)
        return remote(
            held, held, pass_send.at[kind, ka, ks, js], pass_recv.at[kind, ka, ks, js], sibling(js)
        )

    def hand_in(kind, ka, ks, js):
        other = sub_behind(sub, js)
        held = target(kind, behind(ka) * group + sub_behind(other, ks), other)
        return remote(
            held, held, pass_send.at[kind, ka, ks, js], pass_recv.at[kind, ka, ks, js], sibling(js)
        )

    def sib(kind, js):
        return remote(
            source(kind, head, None), target(kind, me, None), sib_send.at[kind, js],
            sib_recv.at[kind, js], sibling(js)
        )

    def sib_in(kind, js):
        return remote(
            source(kind, head, None), target(kind, head * group + sub_behind(sub, js), None),
            sib_send.at[kind, js], sib_recv.at[kind, js], sibling(js)
        )

    def local(kind):
        return pltpu.make_async_copy(
            source(kind, head, None), target(kind, me, None), local_sem.at[kind]
        )

    def launch(kind):
        for ka in range(1, heads):
            for ks in range(group):
                first(kind, ka, ks).start()
        for js in range(1, group):
            sib(kind, js).start()
        local(kind).start()

    def relay(kind):
        for ka in range(1, heads):
            for ks in range(group):
                first_in(kind, ka, ks).wait_recv()
                for js in range(1, group):
                    hand(kind, ka, ks, js).start()

    def settle(kind):
        local(kind).wait()
        for js in range(1, group):
            sib_in(kind, js).wait_recv()
            for ka in range(1, heads):
                for ks in range(group):
                    hand_in(kind, ka, ks, js).wait_recv()

    for k in range(1, narrow):
        tok(k).start()
    held_routes[...] = jnp.zeros_like(held_routes)
    held_routes[0:2, :] = routes_ref[...]
    for k in range(1, wide):
        rt(k).start()
    launch(0)
    launch(1)
    routes_out[me] = held_routes[...]
    held_tokens[depth] = tokens_ref[...]
    for k in range(1, narrow):
        tok_in(k).wait_recv()
    squares = jnp.zeros((block, 1), F32)
    for k in range(narrow):
        floats = held_tokens[k].astype(F32)
        squares = squares + jnp.sum(floats * floats, axis=1, keepdims=True)
    inverse = lax.rsqrt(squares / (narrow * features) + EPS)
    for k in range(narrow):
        at = slice(k * features, (k + 1) * features)
        normed_out[head, :, at] = (
            held_tokens[k].astype(F32) * inverse * gain_ref[at].astype(F32)[None, :]
        ).astype(BF16)

    square = heads == 4
    half = block // 2
    if square:
        x, y = lax.rem(head, 2), lax.div(head, 2)
        neighbour = [y * 2 + 1 - x, (1 - y) * 2 + x]
        far = (1 - y) * 2 + 1 - x

    def near(side, piece):
        held = normed_out.at[head, pl.ds(piece * half, half), :]
        return remote(
            held, held, near_send.at[side, piece], near_recv.at[side, piece],
            (neighbour[side] * group + sub, depth)
        )

    def near_in(side, piece):
        held = normed_out.at[neighbour[side], pl.ds(piece * half, half), :]
        return remote(
            held, held, near_send.at[side, piece], near_recv.at[side, piece],
            (neighbour[side] * group + sub, depth)
        )

    def onward(piece):
        held = normed_out.at[neighbour[piece], pl.ds(piece * half, half), :]
        return remote(
            held, held, near_send.at[2, piece], near_recv.at[2, piece],
            (neighbour[1 - piece] * group + sub, depth)
        )

    def onward_in(piece):
        held = normed_out.at[far, pl.ds(piece * half, half), :]
        return remote(
            held, held, near_send.at[2, piece], near_recv.at[2, piece],
            (neighbour[1 - piece] * group + sub, depth)
        )

    def straight(ka):
        held = normed_out.at[head]
        return remote(
            held, held, near_send.at[0, ka], near_recv.at[0, ka], (ahead(ka) * group + sub, depth)
        )

    def straight_in(ka):
        held = normed_out.at[behind(ka)]
        return remote(
            held, held, near_send.at[0, ka], near_recv.at[0, ka], (behind(ka) * group + sub, depth)
        )

    if square:
        for turn in range(2):
            for side in range(2):
                near(side, (side + turn) % 2).start()
    else:
        for ka in range(1, heads):
            straight(ka).start()
    launch(2)
    relay(0)
    settle(0)

    def keys_values(strand):
        total = lax.dot_general(
            normed_out[strand], held_kvw[...], NT, preferred_element_type=F32
        )
        kv_out[sub, strand] = total.astype(BF16)

    def queries_of(strand):
        normed = normed_out[strand]
        logits = lax.dot_general(normed, router_ref[...], NT, preferred_element_type=F32)
        expert_at = lax.broadcasted_iota(jnp.int32, logits.shape, 1)
        route_a, route_b = route_columns(routes_out[strand * group + sub])
        logit_a = jnp.sum(jnp.where(expert_at == route_a, logits, 0.0), axis=1, keepdims=True)
        logit_b = jnp.sum(jnp.where(expert_at == route_b, logits, 0.0), axis=1, keepdims=True)
        top = jnp.maximum(logit_a, logit_b)
        up_a, up_b = jnp.exp(logit_a - top), jnp.exp(logit_b - top)
        gates_out[strand, :block] = up_a / (up_a + up_b)
        gates_out[strand, block:] = up_b / (up_a + up_b)
        every = lax.dot_general(normed, held_query[...], NT, preferred_element_type=F32)
        parts = [every[:, e * H:(e + 1) * H] for e in range(E)]
        queries_out[strand, :block] = pick(route_a, parts).astype(BF16)
        queries_out[strand, block:] = pick(route_b, parts).astype(BF16)

    def kv_pair(k, strand, js):
        held = kv_out.at[sub, strand]
        return remote(held, held, kv_send.at[k, js], kv_recv.at[k, js], sibling(js))

    def kv_pair_in(k, strand, js):
        held = kv_out.at[sub_behind(sub, js), strand]
        return remote(held, held, kv_send.at[k, js], kv_recv.at[k, js], sibling(js))

    if square:
        order = [head, neighbour[0], neighbour[1], far]
    else:
        order = [behind(ka) for ka in range(heads)]

    def strand_done(k):
        keys_values(order[k])
        for js in range(1, group):
            kv_pair(k, order[k], js).start()

    strand_done(0)
    relay(1)
    if square:
        for piece in range(2):
            near_in(piece, piece).wait_recv()
            onward(piece).start()
        for side in range(2):
            near_in(side, 1 - side).wait_recv()
            strand_done(1 + side)
    else:
        for ka in range(1, heads):
            straight_in(ka).wait_recv()
            strand_done(ka)
    settle(1)
    for k in range(1, wide):
        rt_in(k).wait_recv()
    if square:
        def early(k, none):
            queries_of(jnp.where(k == 0, head, jnp.where(k == 1, neighbour[0], neighbour[1])))

        lax.fori_loop(0, 3, early, None)
    else:
        lax.fori_loop(0, heads, lambda k, none: queries_of(k), None)
    relay(2)
    if square:
        for piece in range(2):
            onward_in(piece).wait_recv()
        strand_done(3)
        queries_of(far)
    settle(2)
    for k in range(heads):
        for js in range(1, group):
            kv_pair_in(k, order[k], js).wait_recv()

    for k in range(1, narrow):
        tok(k).wait_send()
    for k in range(1, wide):
        rt(k).wait_send()
    for kind in range(3):
        for js in range(1, group):
            sib(kind, js).wait_send()
        for ka in range(1, heads):
            for ks in range(group):
                first(kind, ka, ks).wait_send()
                for js in range(1, group):
                    hand(kind, ka, ks, js).wait_send()
    if square:
        for side in range(2):
            for piece in range(2):
                near(side, piece).wait_send()
        for piece in range(2):
            onward(piece).wait_send()
    else:
        for ka in range(1, heads):
            straight(ka).wait_send()
    for k in range(heads):
        for js in range(1, group):
            kv_pair(k, order[k], js).wait_send()


def finish_kernel(
    wide, narrow, group, attended_ref, weight_ref, routes_ref, out_ref,
    gathered, parts, got, mine, final,
    ring_send, ring_recv, pair_send, pair_recv, pass_send, pass_recv,
    deep_send, deep_recv, turn_send, turn_recv
):
    heads = wide // group
    ratio = wide // narrow
    block = attended_ref.shape[2]
    columns = weight_ref.shape[1]
    me, depth = lax.axis_index("wide"), lax.axis_index("narrow")
    head, sub = lax.div(me, group), lax.rem(me, group)
    turned = lax.div(me, ratio)
    lane = lax.rem(me, ratio)

    for k in range(1, wide):
        greet((lax.rem(me + k, wide), depth))
    for k in range(1, narrow):
        greet((me, lax.rem(depth + k, narrow)))
    for u in range(ratio):
        @pl.when(jnp.logical_or(ratio * depth + u != me, turned != depth))
        def _():
            greet((ratio * depth + u, turned))
    own_turn = (turned == depth).astype(jnp.int32)
    pl.semaphore_wait(pltpu.get_barrier_semaphore(), wide - 1 + narrow - 1 + ratio - own_turn)

    strand_at = [lax.rem(depth + 1 + k, heads) for k in range(heads)]
    sibling = [head * group + lax.rem(sub + ks, group) for ks in range(group)]

    square = heads == 4 and attended_ref.shape[1] == 2
    if square:
        x, y = lax.rem(head, 2), lax.div(head, 2)
        neighbour = [y * 2 + 1 - x, (1 - y) * 2 + x]
        origin = [head] + neighbour + [(1 - y) * 2 + 1 - x]
    else:
        origin = [lax.rem(head + heads - ka, heads) for ka in range(heads)]

    def near(k, side, piece):
        i = strand_at[k]
        return remote(
            attended_ref.at[i, piece], gathered.at[head, sub, i, piece],
            ring_send.at[k, side, piece], ring_recv.at[k, side, piece],
            (neighbour[side] * group + sub, depth)
        )

    def near_in(k, side, piece):
        i = strand_at[k]
        return remote(
            attended_ref.at[i, piece], gathered.at[neighbour[side], sub, i, piece],
            ring_send.at[k, side, piece], ring_recv.at[k, side, piece],
            (neighbour[side] * group + sub, depth)
        )

    def onward(k, piece):
        held = gathered.at[neighbour[piece], sub, strand_at[k], piece]
        return remote(
            held, held, ring_send.at[k, 2, piece], ring_recv.at[k, 2, piece],
            (neighbour[1 - piece] * group + sub, depth)
        )

    def onward_in(k, piece):
        held = gathered.at[origin[3], sub, strand_at[k], piece]
        return remote(
            held, held, ring_send.at[k, 2, piece], ring_recv.at[k, 2, piece],
            (neighbour[1 - piece] * group + sub, depth)
        )

    def ring(k, ka):
        i = strand_at[k]
        return remote(
            attended_ref.at[i], gathered.at[head, sub, i], ring_send.at[k, 0, ka],
            ring_recv.at[k, 0, ka], (lax.rem(head + ka, heads) * group + sub, depth)
        )

    def ring_in(k, ka):
        i = strand_at[k]
        return remote(
            attended_ref.at[i], gathered.at[origin[ka], sub, i], ring_send.at[k, 0, ka],
            ring_recv.at[k, 0, ka], (origin[ka] * group + sub, depth)
        )

    def pair(k, ks):
        i = strand_at[k]
        return remote(
            attended_ref.at[i], gathered.at[head, sub, i],
            pair_send.at[k, ks], pair_recv.at[k, ks], (sibling[ks], depth)
        )

    def pair_in(k, ks):
        i = strand_at[k]
        return remote(
            attended_ref.at[i], gathered.at[head, lax.rem(sub + group - ks, group), i],
            pair_send.at[k, ks], pair_recv.at[k, ks], (sibling[ks], depth)
        )

    def hand(k, ka, ks):
        i = strand_at[k]
        held = gathered.at[origin[ka], sub, i]
        return remote(held, held, pass_send.at[k, ka, ks], pass_recv.at[k, ka, ks], (sibling[ks], depth))

    def hand_in(k, ka, ks):
        i = strand_at[k]
        held = gathered.at[origin[ka], lax.rem(sub + group - ks, group), i]
        return remote(held, held, pass_send.at[k, ka, ks], pass_recv.at[k, ka, ks], (sibling[ks], depth))

    def launch(k):
        if square:
            for round in range(2):
                for side in range(2):
                    near(k, side, (side + round) % 2).start()
        else:
            for ka in range(1, heads):
                ring(k, ka).start()
        for ks in range(1, group):
            pair(k, ks).start()

    at_first = 2 if square else heads
    for k in range(at_first):
        launch(k)
    for k in range(heads):
        gathered[head, sub, strand_at[k]] = attended_ref[strand_at[k]]

    def give(k, ka):
        for ks in range(1, group):
            hand(k, ka, ks).start()

    def stage(k):
        if square:
            for piece in range(2):
                near_in(k, piece, piece).wait_recv()
                onward(k, piece).start()
            for side in range(2):
                near_in(k, side, 1 - side).wait_recv()
                give(k, 1 + side)
        else:
            for ka in range(1, heads):
                ring_in(k, ka).wait_recv()
                give(k, ka)
        if at_first + k < heads:
            launch(at_first + k)

    def stage_far(k):
        if square:
            for piece in range(2):
                onward_in(k, piece).wait_recv()
            give(k, 3)

    def arrive(k):
        for ks in range(1, group):
            pair_in(k, ks).wait_recv()
            for ka in range(1, heads):
                hand_in(k, ka, ks).wait_recv()

    def project(which):
        route_a, route_b = route_columns(routes_ref[which])
        total = jnp.zeros((block, columns), F32)
        for h in range(heads):
            first = gathered[h, lax.rem(which, group), lax.div(which, group), 0]
            second = gathered[h, lax.rem(which, group), lax.div(which, group), 1]
            nothing = jnp.zeros_like(first)
            padded = jnp.concatenate(
                [
                    jnp.where(route_a == e, first, jnp.where(route_b == e, second, nothing))
                    for e in range(E)
                ],
                axis=1,
            )
            total = total + jnp.dot(
                padded, weight_ref[h * E * H:(h + 1) * E * H, :], preferred_element_type=F32
            )
        return total

    def deep(k):
        to = lax.rem(depth + 1 + k, narrow)
        return remote(parts.at[k], got.at[k], deep_send.at[k], deep_recv.at[k], (me, to))

    one_each = narrow == heads
    if one_each:
        stage(0)
    else:
        for k in range(heads):
            stage(k)
        for k in range(heads):
            stage_far(k)
            arrive(k)
    owned = []
    for k in range(narrow):
        if one_each:
            stage_far(k)
            if k + 1 < heads:
                stage(k + 1)
            arrive(k)
        quarter = lax.rem(depth + 1 + k, narrow)
        for u in range(ratio):
            total = project(quarter * ratio + u)
            if k < narrow - 1:
                parts[k, u] = total.astype(BF16)
            else:
                owned.append(total)
        if k < narrow - 1:
            deep(k).start()
    for k in range(narrow - 1):
        deep(k).wait_recv()
    for u in range(ratio):
        total = owned[u]
        for k in range(narrow - 1):
            total = total + got[k, u].astype(F32)
        mine[u] = total.astype(BF16)

    def turn(u):
        return remote(
            mine.at[u], final.at[lane], turn_send.at[u], turn_recv.at[lane],
            (ratio * depth + u, turned)
        )

    def turn_in(u):
        return remote(
            mine.at[u], final.at[u], turn_send.at[u], turn_recv.at[u],
            (ratio * depth + u, turned)
        )

    for u in range(ratio):
        apart = jnp.logical_or(ratio * depth + u != me, turned != depth)

        @pl.when(apart)
        def _():
            turn(u).start()

        @pl.when(jnp.logical_not(apart))
        def _():
            final[lane] = mine[u]

    for u in range(ratio):
        apart = jnp.logical_or(ratio * depth + u != me, turned != depth)

        @pl.when(apart)
        def _():
            turn_in(u).wait_recv()

        out_ref[:, u * columns:(u + 1) * columns] = final[u]

    for k in range(heads):
        if square:
            for piece in range(2):
                for side in range(2):
                    near(k, side, piece).wait_send()
                onward(k, piece).wait_send()
        for ka in range(1, heads):
            if not square:
                ring(k, ka).wait_send()
            for ks in range(1, group):
                hand(k, ka, ks).wait_send()
        for ks in range(1, group):
            pair(k, ks).wait_send()
    for k in range(narrow - 1):
        deep(k).wait_send()
    for u in range(ratio):
        @pl.when(jnp.logical_or(ratio * depth + u != me, turned != depth))
        def _():
            turn(u).wait_send()


def on_device(
    wide,
    narrow,
    tokens,
    norm_gain,
    router,
    routes,
    kv_weight,
    query_weight,
    out_weight,
    prefix_cache,
    suffix_lengths,
    prefix_lengths,
):
    block = tokens.shape[0]
    width = router.shape[0]
    heads = kv_weight.shape[0] // (2 * H)
    group = wide // heads
    strands = wide // group
    columns = width // wide
    slots = prefix_cache.shape[0]
    sub = lax.rem(lax.axis_index("wide"), group)
    smem = pl.BlockSpec(memory_space=pltpu.SMEM)
    in_vmem = pl.BlockSpec(memory_space=pltpu.VMEM)
    anywhere = pl.BlockSpec(memory_space=pl.ANY)
    dma = pltpu.SemaphoreType.DMA
    queries, gates, cache, kv, routes_all = pl.pallas_call(
        functools.partial(prepare_kernel, wide, narrow, group),
        out_shape=[
            jax.ShapeDtypeStruct((strands, 2 * block, H), BF16),
            jax.ShapeDtypeStruct((strands, 2 * block, 1), F32),
            jax.ShapeDtypeStruct((wide * slots, 2 * H), BF16),
            jax.ShapeDtypeStruct((group, strands, block, 2 * H), BF16),
            jax.ShapeDtypeStruct((wide, 8, block), jnp.int32),
        ],
        in_specs=[in_vmem] * 4 + [anywhere] * 3,
        out_specs=[in_vmem] * 5,
        scratch_shapes=[
            pltpu.VMEM((narrow,) + tokens.shape, BF16),
            pltpu.VMEM((strands, block, width), BF16),
            pltpu.VMEM((2 * H, width), BF16),
            pltpu.VMEM((E * H, width), BF16),
            pltpu.VMEM((8, block), jnp.int32),
            dma((narrow,)),
            dma((narrow,)),
            dma((wide,)),
            dma((wide,)),
            dma((3, heads, group)),
            dma((3, heads, group)),
            dma((3, heads, group, group)),
            dma((3, heads, group, group)),
            dma((3, group)),
            dma((3, group)),
            dma((3, max(2, heads))),
            dma((3, max(2, heads))),
            dma((heads, group)),
            dma((heads, group)),
            dma((3,)),
        ],
        compiler_params=pltpu.CompilerParams(
            vmem_limit_bytes=56 * 1024 * 1024, collective_id=2, has_side_effects=True
        ),
        name="prepare",
    )(
        tokens,
        norm_gain,
        jnp.transpose(routes),
        jnp.transpose(router),
        kv_weight,
        query_weight,
        prefix_cache,
    )
    attended = pl.pallas_call(
        functools.partial(attend_kernel, group),
        out_shape=jax.ShapeDtypeStruct((strands, 2, block, H), BF16),
        in_specs=[smem] * 3 + [in_vmem] * 4,
        out_specs=in_vmem,
        compiler_params=pltpu.CompilerParams(vmem_limit_bytes=56 * 1024 * 1024),
        name="attend",
    )(
        suffix_lengths,
        prefix_lengths,
        sub[None],
        queries,
        gates,
        cache,
        kv.reshape(wide * block, 2 * H),
    )
    ratio = wide // narrow
    return pl.pallas_call(
        functools.partial(finish_kernel, wide, narrow, group),
        out_shape=jax.ShapeDtypeStruct((block, ratio * columns), BF16),
        in_specs=[in_vmem] * 3,
        out_specs=in_vmem,
        scratch_shapes=[
            pltpu.VMEM((heads, group, strands, 2, block, H), BF16),
            pltpu.VMEM((narrow - 1, ratio, block, columns), BF16),
            pltpu.VMEM((narrow - 1, ratio, block, columns), BF16),
            pltpu.VMEM((ratio, block, columns), BF16),
            pltpu.VMEM((ratio, block, columns), BF16),
            dma((heads, 3, max(2, heads))),
            dma((heads, 3, max(2, heads))),
            dma((heads, group)),
            dma((heads, group)),
            dma((heads, heads, group)),
            dma((heads, heads, group)),
            dma((narrow,)),
            dma((narrow,)),
            dma((ratio,)),
            dma((ratio,)),
        ],
        compiler_params=pltpu.CompilerParams(
            vmem_limit_bytes=56 * 1024 * 1024, collective_id=1, has_side_effects=True
        ),
        name="finish",
    )(attended, out_weight, routes_all)


def solution(mesh):
    placed = (
        P("wide", "narrow"),
        P(),
        P(),
        P("wide", None),
        P("narrow", "wide"),
        P("narrow", "wide"),
        P("narrow", "wide"),
        P("wide", "narrow"),
        P(),
        P(),
    )
    return jax.shard_map(
        functools.partial(on_device, mesh.shape["wide"], mesh.shape["narrow"]),
        mesh=mesh,
        in_specs=placed,
        out_specs=P("wide", "narrow"),
        check_vma=False,
    )
```
